32 devices in a mesh: row: 8 (over y, x, core), col: 4 (over z).
Axes of the slice: x: 2, y: 2, z: 4, core: 2. Of those that a mesh axis runs over, the one named last changes fastest.
Arguments:
- queries: bfloat16 [2048, 8192], P('row', 'col'), may hold values from -96 to 96
- keys: bfloat16 [2048, 1024], P('row'), may hold values from -4.05 to 4.05
- values: bfloat16 [2048, 1024], P('row'), may hold values from -4 to 4
- grad_attn: bfloat16 [2048, 8192], P('row', 'col'), may hold values from -12 to 12
- segment_ids: int32 [2048], replicated, may hold values from 0 to 3, as said below
- q_weight: bfloat16 [8192, 8192], P('row', 'col'), may hold values from -0.0625 to 0.0625
Outputs:
- input_grad: bfloat16 [2048, 8192], P('row', 'col')
- key_grad: bfloat16 [2048, 1024], P('row')
- value_grad: bfloat16 [2048, 1024], P('row')
The draws below stay inside these ranges and needn't reach their ends.
Inputs may be any that keep to these rules, and one draw needn't show every extreme that they name: `segment_ids`: document numbers never fall along the sequence; a document holds 1 to 1024 positions; the last document holds exactly the last 1024 positions.
All inputs are finite; a program needn't handle non-finite values.
Results may differ from the reference program's by a relative error of at most 0.015.
Values may be sent and summed in bfloat16 or wider, within the bound.
No kernel may reach another device: no remote copies, remote signals or barrier semaphores. Data moves between devices by JAX's collectives and lax.ppermute only.
A program may use at most 128 MiB of HBM per device.

```python
import math
import jax
import jax.numpy as jnp
from jax import lax

D = 8192
H = 64
KVH = 8
HD = 128
TOK_DEV = 256
TOKENS = 2048


def draw_both(key):
    key_keys = jax.random.fold_in(key, 101)
    key_query = jax.random.fold_in(key, 202)
    base_keys = jnp.clip(jax.random.normal(key_keys, (TOKENS, KVH * HD), jnp.float32), -4.0, 4.0)
    base_query = jnp.clip(jax.random.normal(key_query, (TOKENS, H * HD), jnp.float32), -4.0, 4.0)
    keys_out = base_keys
    query_out = base_query
    return (query_out, keys_out)


def draw_queries(key, part):
    return draw_both(key)[0].astype(jnp.bfloat16)


def draw_keys(key, part):
    return draw_both(key)[1].astype(jnp.bfloat16)


def draw_segment_ids(key, part):
    half_len = TOKENS // 2
    order = jax.random.permutation(jax.random.fold_in(key, 404), half_len - 1)
    first_cut = jnp.minimum(order[0], order[1]).astype(jnp.int32) + 1
    second_cut = jnp.maximum(order[0], order[1]).astype(jnp.int32) + 1
    places = jnp.arange(TOKENS, dtype=jnp.int32)
    seg = (places >= first_cut).astype(jnp.int32) + (places >= second_cut).astype(jnp.int32) + (places >= half_len).astype(jnp.int32)
    return seg.astype(jnp.int32)


def level_of(rng, shape, shards, smallest, top_value):
    def one(axis_at, blocks):
        heights = jax.random.uniform(jax.random.fold_in(jax.random.fold_in(rng, 6), axis_at), (blocks,), jnp.float32, smallest / len(shards), top_value / len(shards))
        return jnp.repeat(jnp.exp(heights), shape[axis_at] // blocks).reshape((-1,) + (1,) * (len(shape) - axis_at - 1))

    loudness = one(*shards[0])
    for cut in shards[1:]:
        loudness = loudness * one(*cut)
    return loudness


def noise(key, shape, scale, reach, split=(), kind=jnp.bfloat16):
    array = scale * jax.random.normal(key, shape, jnp.float32)
    if split:
        array = array * level_of(key, shape, split, -0.22, 0.18)
    return jnp.clip(array, -reach, reach).astype(kind)


def setup_inputs(seed: int = 0) -> dict:
    arg_keys = jax.random.split(jax.random.key(seed), 7)
    queries = draw_queries(jax.random.fold_in(arg_keys[6], 71), 0)
    keys = draw_keys(jax.random.fold_in(arg_keys[6], 71), 0)
    values = noise(arg_keys[2], (TOKENS, KVH * HD), 1.0, 4.0, ((0, 8),))
    grad_attn = noise(arg_keys[3], (TOKENS, H * HD), 2.0, 12.0, ((0, 8), (1, 4)))
    segment_ids = draw_segment_ids(jax.random.fold_in(arg_keys[6], 71), 0)
    q_weight = noise(arg_keys[5], (H * HD, D), D ** -0.5, 0.0625, ((0, 8), (1, 4)))
    return {"queries": queries, "keys": keys, "values": values, "grad_attn": grad_attn, "segment_ids": segment_ids, "q_weight": q_weight}


def reference(queries, keys, values, grad_attn, segment_ids, q_weight):
    inv_root = 1.0 / math.sqrt(HD)
    group_size = H // KVH
    half_rows = TOK_DEV // 2
    rows_all = jnp.arange(TOKENS, dtype=jnp.int32)
    shard_of = rows_all // TOK_DEV
    local_of = rows_all % TOK_DEV
    places = jnp.where(local_of < half_rows, shard_of * half_rows + local_of, TOKENS - (shard_of + 1) * half_rows + local_of - half_rows).astype(jnp.int32)
    segs = segment_ids[places]
    allowed = (places[None, :] <= places[:, None]) & (segs[None, :] == segs[:, None])
    query_heads = queries.reshape(TOKENS, H, HD).transpose(1, 0, 2)
    grad_heads = grad_attn.reshape(TOKENS, H, HD).transpose(1, 0, 2)
    key_heads = keys.reshape(TOKENS, KVH, HD).transpose(1, 0, 2)
    value_heads = values.reshape(TOKENS, KVH, HD).transpose(1, 0, 2)

    def one_head(head_index):
        query_h = query_heads[head_index]
        grad_h = grad_heads[head_index]
        key_h = key_heads[head_index // group_size]
        value_h = value_heads[head_index // group_size]
        scores = jnp.dot(query_h, key_h.T, preferred_element_type=jnp.float32) * inv_root
        masked = jnp.where(allowed, scores, -jnp.inf)
        row_top = lax.optimization_barrier(jnp.max(masked, axis=1, keepdims=True))
        row_sum = lax.optimization_barrier(jnp.sum(jnp.exp(masked - row_top), axis=1, keepdims=True))
        row_lse = row_top + jnp.log(row_sum)
        softmax_w = jnp.where(allowed, jnp.exp(masked - row_lse), 0.0)
        grad_prob = jnp.dot(grad_h, value_h.T, preferred_element_type=jnp.float32)
        prob_dot = lax.optimization_barrier(jnp.sum(softmax_w * grad_prob, axis=1, keepdims=True))
        dscore = (softmax_w * (grad_prob - prob_dot)).astype(jnp.bfloat16)
        soft_low = softmax_w.astype(jnp.bfloat16)
        query_part = jnp.dot(dscore, key_h, preferred_element_type=jnp.float32) * inv_root
        key_part = jnp.dot(dscore.T, query_h, preferred_element_type=jnp.float32) * inv_root
        value_part = jnp.dot(soft_low.T, grad_h, preferred_element_type=jnp.float32)
        return (query_part, key_part, value_part)
    query_parts, key_parts, value_parts = lax.map(one_head, jnp.arange(H, dtype=jnp.int32))
    key_sum = key_parts.reshape(KVH, group_size, TOKENS, HD).sum(axis=1)
    value_sum = value_parts.reshape(KVH, group_size, TOKENS, HD).sum(axis=1)
    key_grad = key_sum.transpose(1, 0, 2).reshape(TOKENS, KVH * HD).astype(jnp.bfloat16)
    value_grad = value_sum.transpose(1, 0, 2).reshape(TOKENS, KVH * HD).astype(jnp.bfloat16)
    query_grad = query_parts.transpose(1, 0, 2).reshape(TOKENS, H * HD).astype(jnp.bfloat16)
    input_grad = jnp.dot(query_grad, q_weight, preferred_element_type=jnp.float32).astype(jnp.bfloat16)
    return (input_grad, key_grad, value_grad)
```

```python
import functools
import math

import jax
import jax.numpy as jnp
from jax import lax
from jax.experimental import pallas as pl
from jax.experimental.pallas import tpu as pltpu
from jax.sharding import PartitionSpec as P

H = 64
KVH = 8
HD = 128
CHUNKS = 4

NEG = -1e30


def attention_kernel(
    kv_here, per_kv, rows, ranks, relative, me_ref, seg_query, seg_key, q_ref, g_ref, kv_ref,
    dq_ref, dkv_ref, q_rows, g_rows, q_cols, g_cols, s_all, d_all, p_low, d_low, top, total, dots,
):
    half = rows // 2
    width = kv_here * HD
    inv_root = 1.0 / math.sqrt(HD)
    scale = inv_root * math.log2(math.e)
    me = me_ref[0]
    contract_last = (((1,), (1,)), ((), ()))
    dkv_ref[...] = jnp.zeros_like(dkv_ref)
    for g in range(kv_here):
        for side in range(2):
            here = slice(side * half, (side + 1) * half)
            blocks = me + 1 if side == 0 else ranks - me
            steps = (blocks + 1) // 2
            for p in range(per_kv):
                head = slice((g * per_kv + p) * HD, (g * per_kv + p + 1) * HD)
                q_rows[p * half:(p + 1) * half, :] = q_ref[here, head]
                g_rows[p * half:(p + 1) * half, :] = g_ref[here, head]
            q_cols[...] = q_rows[...].T
            g_cols[...] = g_rows[...].T

            def piece(block):
                owner = block if side == 0 else ranks - 1 - block
                return owner ^ me

            def pair(j, first):
                one = kv_ref[piece(2 * j), here, first:first + HD]
                two = kv_ref[piece(2 * j + 1), here, first:first + HD]
                return jnp.concatenate([one, two], axis=0)

            top[...] = jnp.full_like(top, NEG)
            total[...] = jnp.zeros_like(total)
            dots[...] = jnp.zeros_like(dots)

            def scores(j, carry):
                keys = pair(j, g * HD)
                vals = pair(j, width + g * HD)
                query_at = (blocks - 1) * half + lax.broadcasted_iota(jnp.int32, (half, 2 * half), 0)
                key_at = j * 2 * half + lax.broadcasted_iota(jnp.int32, (half, 2 * half), 1)
                segs = seg_key[side * (ranks // 2) + j]
                allowed = (key_at <= query_at) & (segs == seg_query[side])
                bias = jnp.where(allowed, 0.0, NEG)
                for p in range(per_kv):
                    at = slice(p * half, (p + 1) * half)
                    s = lax.dot_general(
                        q_rows[at, :], keys, contract_last, preferred_element_type=jnp.float32
                    )
                    s = s * scale + bias
                    s_all[j, at, :] = s
                    top[at, :] = jnp.maximum(top[at, :], jnp.maximum(s[:, :half], s[:, half:]))
                    d_all[j, at, :] = lax.dot_general(
                        g_rows[at, :], vals, contract_last, preferred_element_type=jnp.float32
                    )
                return carry

            lax.fori_loop(0, steps, scores, 0)
            top[...] = jnp.broadcast_to(jnp.max(top[...], axis=1, keepdims=True), top.shape)

            def sums(j, carry):
                for p in range(per_kv):
                    at = slice(p * half, (p + 1) * half)
                    high = top[at, :]
                    s = s_all[j, at, :]
                    e = jnp.exp2(s - jnp.concatenate([high, high], axis=1))
                    s_all[j, at, :] = e
                    total[at, :] += e[:, :half] + e[:, half:]
                    ed = e * d_all[j, at, :]
                    dots[at, :] += ed[:, :half] + ed[:, half:]
                return carry

            lax.fori_loop(0, steps, sums, 0)
            inverse = 1.0 / jnp.sum(total[...], axis=1, keepdims=True)
            delta = jnp.sum(dots[...], axis=1, keepdims=True) * inverse
            total[...] = jnp.broadcast_to(inverse, total.shape)
            dots[...] = jnp.broadcast_to(delta, dots.shape)
            top[...] = jnp.zeros_like(top)

            def grads(j, carry):
                keys = pair(j, g * HD)
                for p in range(per_kv):
                    at = slice(p * half, (p + 1) * half)
                    inv = total[at, :]
                    dot = dots[at, :]
                    prob = s_all[j, at, :] * jnp.concatenate([inv, inv], axis=1)
                    p_low[at, :] = prob.astype(jnp.bfloat16)
                    shifted = d_all[j, at, :] - jnp.concatenate([dot, dot], axis=1)
                    d_low[at, :] = (prob * shifted).astype(jnp.bfloat16)
                top[...] += jnp.dot(d_low[...], keys, preferred_element_type=jnp.float32)
                key_part = jnp.dot(q_cols[...], d_low[...], preferred_element_type=jnp.float32)
                val_part = jnp.dot(g_cols[...], p_low[...], preferred_element_type=jnp.float32)
                key_part = (key_part * inv_root).T.astype(jnp.bfloat16)
                val_part = val_part.T.astype(jnp.bfloat16)
                for i in range(2):
                    out = piece(2 * j + i)
                    rows_i = slice(i * half, (i + 1) * half)
                    dkv_ref[out, here, g * HD:(g + 1) * HD] = key_part[rows_i, :]
                    dkv_ref[out, here, width + g * HD:width + (g + 1) * HD] = val_part[rows_i, :]
                return carry

            lax.fori_loop(0, steps, grads, 0)
            for p in range(per_kv):
                at = slice(p * half, (p + 1) * half)
                slot = p ^ me if relative else p
                dq_ref[slot, g, here, :] = (top[at, :] * inv_root).astype(jnp.bfloat16)


def attention(me, seg_query, seg_key, queries, grad_attn, kv, kv_here, per_kv, relative):
    ranks, rows = kv.shape[:2]
    half = rows // 2
    stack = per_kv * half
    pairs = ranks // 2
    vmem = pl.BlockSpec(memory_space=pltpu.VMEM)
    return pl.pallas_call(
        functools.partial(attention_kernel, kv_here, per_kv, rows, ranks, relative),
        out_shape=(
            jax.ShapeDtypeStruct((per_kv, kv_here, rows, HD), jnp.bfloat16),
            jax.ShapeDtypeStruct(kv.shape, jnp.bfloat16),
        ),
        in_specs=[pl.BlockSpec(memory_space=pltpu.SMEM)] + [vmem] * 5,
        out_specs=(vmem, vmem),
        scratch_shapes=[
            pltpu.VMEM((stack, HD), jnp.bfloat16),
            pltpu.VMEM((stack, HD), jnp.bfloat16),
            pltpu.VMEM((HD, stack), jnp.bfloat16),
            pltpu.VMEM((HD, stack), jnp.bfloat16),
            pltpu.VMEM((pairs, stack, 2 * half), jnp.float32),
            pltpu.VMEM((pairs, stack, 2 * half), jnp.float32),
            pltpu.VMEM((stack, 2 * half), jnp.bfloat16),
            pltpu.VMEM((stack, 2 * half), jnp.bfloat16),
            pltpu.VMEM((stack, HD), jnp.float32),
            pltpu.VMEM((stack, HD), jnp.float32),
            pltpu.VMEM((stack, HD), jnp.float32),
        ],
        compiler_params=pltpu.CompilerParams(vmem_limit_bytes=40 << 20),
        cost_estimate=pl.CostEstimate(
            flops=20_000_000_000, bytes_accessed=8_000_000, transcendentals=3_000_000
        ),
        name="attention",
    )(me, seg_query, seg_key, queries, grad_attn, kv)


def project_kernel(ranks, order_ref, w_ref, *refs):
    parts, out_ref = refs[:-1], refs[-1]
    lhs = jnp.concatenate([part[...] for part in parts], axis=1)
    rhs = jnp.concatenate([w_ref[order_ref[i]] for i in range(len(parts))], axis=0)
    out = jnp.dot(lhs, rhs, preferred_element_type=jnp.float32)
    out_ref[...] = out.astype(jnp.bfloat16)


def project(order, weights, parts):
    ranks, depth, features = weights.shape
    rows = parts[0].shape[0]
    tile = min(256, features)
    return pl.pallas_call(
        functools.partial(project_kernel, ranks),
        out_shape=jax.ShapeDtypeStruct((rows, features), jnp.bfloat16),
        grid=(features // tile,),
        in_specs=[
            pl.BlockSpec(memory_space=pltpu.SMEM),
            pl.BlockSpec((ranks, depth, tile), lambda n: (0, 0, n)),
        ] + [pl.BlockSpec((rows, depth), lambda n: (0, 0))] * len(parts),
        out_specs=pl.BlockSpec((rows, tile), lambda n: (0, n)),
        compiler_params=pltpu.CompilerParams(vmem_limit_bytes=32 << 20),
        cost_estimate=pl.CostEstimate(
            flops=2 * rows * depth * len(parts) * features,
            bytes_accessed=2 * (rows * (depth * len(parts) + features) + ranks * depth * features),
            transcendentals=0,
        ),
        name="project",
    )(order, weights, *parts)


def across(block, mask):
    ranks = lax.axis_size("row")
    return lax.ppermute(block, "row", [(i, i ^ mask) for i in range(ranks)])


def turned(block, distance):
    count = lax.axis_size("col")
    return lax.ppermute(block, "col", [((i + distance) % count, i) for i in range(count)])


def gather_col(block):
    count = lax.axis_size("col")
    found = {0: block}
    ahead = behind = block
    for k in range(1, (count - 1) // 2 + 1):
        ahead = turned(ahead, 1)
        behind = turned(behind, -1)
        found[k], found[count - k] = ahead, behind
    if count % 2 == 0:
        cut = block.shape[0] // 2
        found[count // 2] = jnp.concatenate(
            [turned(ahead[:cut], 1), turned(behind[cut:], -1)], axis=0
        )
    return [found[k] for k in range(count)]


def added(one, two):
    return (one.astype(jnp.float32) + two.astype(jnp.float32)).astype(jnp.bfloat16)


def scatter_sum(blocks, bits):
    ranks = blocks.shape[0]
    shape = blocks.shape[1:]
    now = blocks.reshape((2,) * bits + shape)
    left = list(range(bits))
    for b in [0]:
        axis = left[::-1].index(b)
        keep = lax.index_in_dim(now, 0, axis, keepdims=False)
        send = lax.index_in_dim(now, 1, axis, keepdims=False)
        now = added(keep, across(send, 1 << b))
        left.remove(b)
    cut = shape[-1] // 2
    done = []
    for part, order in ((now[..., :cut], left), (now[..., cut:], left[::-1])):
        rest = list(left)
        for b in order:
            axis = rest[::-1].index(b)
            keep = lax.index_in_dim(part, 0, axis, keepdims=False)
            send = lax.index_in_dim(part, 1, axis, keepdims=False)
            part = added(keep, across(send, 1 << b))
            rest.remove(b)
        done.append(part)
    return jnp.concatenate(done, axis=-1)


def local(queries, keys, values, grad_attn, segment_ids, q_weight):
    rows = queries.shape[0]
    half = rows // 2
    ranks = lax.axis_size("row")
    count = lax.axis_size("col")
    bits = ranks.bit_length() - 1
    heads_here = queries.shape[1] // HD
    group = H // KVH
    kv_here = max(1, heads_here // group)
    per_kv = heads_here // kv_here
    width = kv_here * HD
    total_rows = ranks * rows
    me = lax.axis_index("row")
    col = lax.axis_index("col")
    kv_first = col * heads_here // group

    mine = jnp.concatenate(
        [
            lax.dynamic_slice_in_dim(keys, kv_first * HD, width, 1),
            lax.dynamic_slice_in_dim(values, kv_first * HD, width, 1),
        ],
        axis=1,
    )
    even = jnp.stack([mine] + [across(mine, d) for d in range(2, ranks, 2)])
    odd = across(even, 1)
    kv = jnp.stack([even, odd], axis=1).reshape(ranks, rows, 2 * width)

    rows_w = q_weight.shape[0]
    depth = rows_w // ranks
    w_cut = q_weight.reshape(ranks, depth, q_weight.shape[1])
    w_blocks = [lax.dynamic_index_in_dim(w_cut, me, 0, keepdims=False)]
    for d in range(1, ranks):
        w_blocks.append(across(lax.dynamic_index_in_dim(w_cut, me ^ d, 0, keepdims=False), d))
    weights = jnp.stack(w_blocks)

    key_segs = segment_ids.reshape(ranks, 1, 2 * half)
    own = segment_ids.reshape(2 * ranks, half)
    query_segs = jnp.stack(
        [
            lax.dynamic_index_in_dim(own, me, 0, keepdims=False),
            lax.dynamic_index_in_dim(own, 2 * ranks - 1 - me, 0, keepdims=False),
        ]
    )[:, :, None]
    direct = per_kv == ranks and depth == HD
    dq, dkv = attention(
        me.reshape(1), query_segs, key_segs, queries, grad_attn, kv, kv_here, per_kv, direct
    )
    per_col = heads_here * HD // rows_w
    if not direct:
        dq = dq.transpose(2, 1, 0, 3).reshape(rows, per_col, ranks, depth)
        dq = dq.transpose(2, 1, 0, 3)[me ^ jnp.arange(ranks)]

    spread = [dq[0]] + [across(dq[d], d) for d in range(1, ranks)]
    tokens = jnp.stack(spread)
    order = jnp.concatenate(
        [me ^ (((col + k) % count) * per_col + jnp.arange(per_col)) for k in range(count)]
    ).astype(jnp.int32)
    step = rows // CHUNKS
    outs = []
    for c in range(CHUNKS):
        chunk = tokens[:, :, c * step:(c + 1) * step, :].transpose(1, 0, 2, 3)
        parts = []
        for found in gather_col(chunk.reshape(per_col, ranks * step, depth).transpose(1, 0, 2).reshape(ranks * step, per_col * depth)):
            parts += [found[:, i * depth:(i + 1) * depth] for i in range(per_col)]
        partial = project(order, weights, parts)
        outs.append(scatter_sum(partial.reshape(ranks, step, -1), bits))
    input_grad = jnp.concatenate(outs, axis=0)

    dkv_mine = scatter_sum(dkv, bits)
    found = gather_col(dkv_mine)
    share = max(1, group // heads_here)
    whole = jnp.stack(found)
    whole = jnp.roll(whole, col, axis=0) if count > 1 else whole
    if share > 1:
        whole = whole.reshape(count // share, share, rows, 2 * width).astype(jnp.float32)
        whole = whole.sum(axis=1).astype(jnp.bfloat16)
    key_grad = whole[..., :width].transpose(1, 0, 2).reshape(rows, KVH * HD)
    value_grad = whole[..., width:].transpose(1, 0, 2).reshape(rows, KVH * HD)
    return (input_grad, key_grad, value_grad)


def solution(mesh):
    placed = (
        P("row", "col"),
        P("row", None),
        P("row", None),
        P("row", "col"),
        P(),
        P("row", "col"),
    )
    return jax.shard_map(
        local,
        mesh=mesh,
        in_specs=placed,
        out_specs=(P("row", "col"), P("row", None), P("row", None)),
        check_vma=False,
    )
```

```python
import functools
import math

import jax
import jax.numpy as jnp
from jax import lax
from jax.experimental import pallas as pl
from jax.experimental.pallas import tpu as pltpu
from jax.sharding import PartitionSpec as P

H = 64
KVH = 8
HD = 128

NEG = -1e30


def attention_kernel(
    per_kv, rows, ranks, me_ref, seg_query, seg_key, q_ref, g_ref, kv_even, kv_odd,
    dq_ref, dkv_even, dkv_odd, q_rows, g_rows, q_cols, g_cols, s_all, d_all, p_low, d_low, top, total, dots,
):
    half = rows // 2
    inv_root = 1.0 / math.sqrt(HD)
    scale = inv_root * math.log2(math.e)
    me = me_ref[0]
    parity = me & 1
    contract_last = (((1,), (1,)), ((), ()))
    dkv_even[...] = jnp.zeros_like(dkv_even)
    dkv_odd[...] = jnp.zeros_like(dkv_odd)
    for side in range(2):
        here = slice(side * half, (side + 1) * half)
        blocks = me + 1 if side == 0 else ranks - me
        steps = (blocks + 1) // 2
        swap = parity if side == 0 else 1 - parity
        for p in range(per_kv):
            head = slice(p * HD, (p + 1) * HD)
            q_rows[p * half:(p + 1) * half, :] = q_ref[here, head]
            g_rows[p * half:(p + 1) * half, :] = g_ref[here, head]
        q_cols[...] = q_rows[...].T
        g_cols[...] = g_rows[...].T

        def slot(j):
            chip = j if side == 0 else ranks // 2 - 1 - j
            return chip ^ (me >> 1)

        def pair(j, first):
            at = slot(j)
            cols = slice(first, first + HD)
            return jnp.concatenate([kv_even[at, here, cols], kv_odd[at, here, cols]], axis=0)

        top[...] = jnp.full_like(top, NEG)
        total[...] = jnp.zeros_like(total)
        dots[...] = jnp.zeros_like(dots)

        def scores(j, carry):
            keys = pair(j, 0)
            vals = pair(j, HD)
            query_at = (blocks - 1) * half + lax.broadcasted_iota(jnp.int32, (half, half), 0)
            bias = []
            for block in (2 * j + swap, 2 * j + 1 - swap):
                key_at = block * half + lax.broadcasted_iota(jnp.int32, (half, half), 1)
                segs = seg_key[side * ranks + block]
                allowed = (key_at <= query_at) & (segs == seg_query[side])
                bias.append(jnp.where(allowed, 0.0, NEG))
            bias = jnp.concatenate(bias, axis=1)
            for p in range(per_kv):
                at = slice(p * half, (p + 1) * half)
                s = lax.dot_general(
                    q_rows[at, :], keys, contract_last, preferred_element_type=jnp.float32
                )
                s = s * scale + bias
                s_all[j, at, :] = s
                top[at, :] = jnp.maximum(top[at, :], jnp.maximum(s[:, :half], s[:, half:]))
                d_all[j, at, :] = lax.dot_general(
                    g_rows[at, :], vals, contract_last, preferred_element_type=jnp.float32
                )
            return carry

        lax.fori_loop(0, steps, scores, 0)
        top[...] = jnp.broadcast_to(jnp.max(top[...], axis=1, keepdims=True), top.shape)

        def sums(j, carry):
            for p in range(per_kv):
                at = slice(p * half, (p + 1) * half)
                high = top[at, :]
                s = s_all[j, at, :]
                e = jnp.exp2(s - jnp.concatenate([high, high], axis=1))
                s_all[j, at, :] = e
                total[at, :] += e[:, :half] + e[:, half:]
                ed = e * d_all[j, at, :]
                dots[at, :] += ed[:, :half] + ed[:, half:]
            return carry

        lax.fori_loop(0, steps, sums, 0)
        inverse = 1.0 / jnp.sum(total[...], axis=1, keepdims=True)
        delta = jnp.sum(dots[...], axis=1, keepdims=True) * inverse
        total[...] = jnp.broadcast_to(inverse, total.shape)
        dots[...] = jnp.broadcast_to(delta, dots.shape)
        top[...] = jnp.zeros_like(top)

        def grads(j, carry):
            keys = pair(j, 0)
            for p in range(per_kv):
                at = slice(p * half, (p + 1) * half)
                inv = total[at, :]
                dot = dots[at, :]
                prob = s_all[j, at, :] * jnp.concatenate([inv, inv], axis=1)
                p_low[at, :] = prob.astype(jnp.bfloat16)
                shifted = d_all[j, at, :] - jnp.concatenate([dot, dot], axis=1)
                d_low[at, :] = (prob * shifted).astype(jnp.bfloat16)
            top[...] += jnp.dot(d_low[...], keys, preferred_element_type=jnp.float32)
            key_part = jnp.dot(q_cols[...], d_low[...], preferred_element_type=jnp.float32)
            val_part = jnp.dot(g_cols[...], p_low[...], preferred_element_type=jnp.float32)
            key_part = (key_part * inv_root).T.astype(jnp.bfloat16)
            val_part = val_part.T.astype(jnp.bfloat16)
            at = slot(j)
            dkv_even[at, here, :HD] = key_part[:half, :]
            dkv_odd[at, here, :HD] = key_part[half:, :]
            dkv_even[at, here, HD:] = val_part[:half, :]
            dkv_odd[at, here, HD:] = val_part[half:, :]
            return carry

        lax.fori_loop(0, steps, grads, 0)
        grad = (top[...] * inv_root).astype(jnp.bfloat16)
        for p in range(per_kv):
            part, at = divmod(p, per_kv // 2)
            dq_ref[0, part, here, at * HD:(at + 1) * HD] = grad[p * half:(p + 1) * half, :]


def attention(me, seg_query, seg_key, queries, grad_attn, kv_even, kv_odd, kv_here, per_kv):
    pairs, rows, width = kv_even.shape
    ranks = 2 * pairs
    half = rows // 2
    stack = per_kv * half
    vmem = pl.BlockSpec(memory_space=pltpu.VMEM)
    heads = pl.BlockSpec((rows, per_kv * HD), lambda g: (0, g))
    kv_spec = pl.BlockSpec((pairs, rows, 2 * HD), lambda g: (0, 0, g))
    wide = per_kv // 2 * HD
    return pl.pallas_call(
        functools.partial(attention_kernel, per_kv, rows, ranks),
        out_shape=[jax.ShapeDtypeStruct((kv_here, 2, rows, wide), jnp.bfloat16)]
        + [jax.ShapeDtypeStruct((pairs, rows, width), jnp.bfloat16)] * 2,
        grid=(kv_here,),
        in_specs=[pl.BlockSpec(memory_space=pltpu.SMEM), vmem, vmem, heads, heads, kv_spec, kv_spec],
        out_specs=[pl.BlockSpec((1, 2, rows, wide), lambda g: (g, 0, 0, 0)), kv_spec, kv_spec],
        scratch_shapes=[
            pltpu.VMEM((stack, HD), jnp.bfloat16),
            pltpu.VMEM((stack, HD), jnp.bfloat16),
            pltpu.VMEM((HD, stack), jnp.bfloat16),
            pltpu.VMEM((HD, stack), jnp.bfloat16),
            pltpu.VMEM((pairs, stack, 2 * half), jnp.float32),
            pltpu.VMEM((pairs, stack, 2 * half), jnp.float32),
            pltpu.VMEM((stack, 2 * half), jnp.bfloat16),
            pltpu.VMEM((stack, 2 * half), jnp.bfloat16),
            pltpu.VMEM((stack, HD), jnp.float32),
            pltpu.VMEM((stack, HD), jnp.float32),
            pltpu.VMEM((stack, HD), jnp.float32),
        ],
        compiler_params=pltpu.CompilerParams(vmem_limit_bytes=32 << 20),
        cost_estimate=pl.CostEstimate(
            flops=14_000_000_000, bytes_accessed=8_000_000, transcendentals=3_000_000
        ),
        name="attention",
    )(me, seg_query, seg_key, queries, grad_attn, kv_even, kv_odd)


def project_kernel(slot_ref, *refs):
    even_ref, odd_ref, lhs = refs[-3:]
    count = lhs.shape[0]
    weights, parts = refs[:count], refs[count:-3]
    blocks, step, features = even_ref.shape
    for k in range(count):
        lhs[slot_ref[k]] = parts[k][...].reshape(lhs.shape[1:])
    tile = min(256, features)

    def columns(n, carry):
        at = pl.ds(pl.multiple_of(n * tile, tile), tile)
        out = jnp.dot(lhs[0], weights[0][:, at], preferred_element_type=jnp.float32)
        for k in range(1, count):
            out += jnp.dot(lhs[k], weights[k][:, at], preferred_element_type=jnp.float32)
        out = out.astype(jnp.bfloat16).reshape(2 * blocks, step, tile)
        for i in range(blocks):
            even_ref[i, :, at] = out[2 * i]
            odd_ref[i, :, at] = out[2 * i + 1]
        return carry

    lax.fori_loop(0, features // tile, columns, 0)


def project(slots, weights, parts):
    count = len(weights)
    group, step, depth = parts[0].shape
    features = weights[0].shape[1]
    smem = pl.BlockSpec(memory_space=pltpu.SMEM)
    vmem = pl.BlockSpec(memory_space=pltpu.VMEM)
    return pl.pallas_call(
        project_kernel,
        out_shape=[jax.ShapeDtypeStruct((group // 2, step, features), jnp.bfloat16)] * 2,
        in_specs=[smem] + [vmem] * (count + len(parts)),
        out_specs=[vmem, vmem],
        scratch_shapes=[pltpu.VMEM((count, group * step, depth), jnp.bfloat16)],
        compiler_params=pltpu.CompilerParams(vmem_limit_bytes=32 << 20),
        cost_estimate=pl.CostEstimate(
            flops=2 * group * step * depth * count * features,
            bytes_accessed=2 * (group * step * features + count * depth * features),
            transcendentals=0,
        ),
        name="project",
    )(slots, *weights, *parts)


def columns_kernel(col_ref, *refs):
    parts, outs = refs[:-2], refs[-2:]
    count = len(parts)
    heads = parts[0].shape[1] // (2 * HD)
    for k in range(count):
        where = lax.rem(col_ref[0] + k, count) * heads
        for i in range(2 * heads):
            at = pl.ds(pl.multiple_of((where + i // 2) * HD, HD), HD)
            outs[i % 2][:, at] = parts[k][:, i * HD:(i + 1) * HD]


def by_column(col, parts):
    rows, width = parts[0].shape
    vmem = pl.BlockSpec(memory_space=pltpu.VMEM)
    return pl.pallas_call(
        columns_kernel,
        out_shape=[jax.ShapeDtypeStruct((rows, len(parts) * width // 2), jnp.bfloat16)] * 2,
        in_specs=[pl.BlockSpec(memory_space=pltpu.SMEM)] + [vmem] * len(parts),
        out_specs=[vmem, vmem],
        name="by_column",
    )(col, *parts)


def across(block, mask):
    ranks = lax.axis_size("row")
    return lax.ppermute(block, "row", [(i, i ^ mask) for i in range(ranks)])


def turned(block, distance):
    count = lax.axis_size("col")
    return lax.ppermute(block, "col", [((i + distance) % count, i) for i in range(count)])


def opposite(ahead, behind):
    cut = ahead.shape[0] // 2
    return turned(ahead[:cut], 1), turned(behind[cut:], -1)


def added(one, two):
    return (one.astype(jnp.float32) + two.astype(jnp.float32)).astype(jnp.bfloat16)


def tied(*arrays):
    return lax.optimization_barrier(arrays)


def local(queries, keys, values, grad_attn, segment_ids, q_weight):
    rows = queries.shape[0]
    half = rows // 2
    ranks = lax.axis_size("row")
    count = lax.axis_size("col")
    heads_here = queries.shape[1] // HD
    group = H // KVH
    kv_here = max(1, heads_here // group)
    per_kv = heads_here // kv_here
    me = lax.axis_index("row")
    col = lax.axis_index("col")
    kv_first = col * heads_here // group

    mine = []
    for g in range(kv_here):
        for array in (keys, values):
            mine.append(lax.dynamic_slice_in_dim(array, (kv_first + g) * HD, HD, 1))
    mine = jnp.concatenate(mine, axis=1)
    kv_even = jnp.stack([mine] + [across(mine, d) for d in range(2, ranks, 2)])
    kv_odd = across(kv_even, 1)

    rows_w = q_weight.shape[0]
    key_segs = segment_ids.reshape(2 * ranks, 1, half)
    own = segment_ids.reshape(2 * ranks, half)
    query_segs = jnp.stack(
        [
            lax.dynamic_index_in_dim(own, me, 0, keepdims=False),
            lax.dynamic_index_in_dim(own, 2 * ranks - 1 - me, 0, keepdims=False),
        ]
    )[:, :, None]
    special = ranks == 8 and count == 4
    if special:
        cut = q_weight.reshape(4, rows_w // 4, -1)
        side = (me >> 1) & 1
        quarters = [
            lax.dynamic_index_in_dim(cut, 2 * at + i, 0, keepdims=False)
            for at in (side, 1 - side) for i in range(2)
        ]
        kv_even, kv_odd, *quarters = tied(kv_even, kv_odd, *quarters)
    dq, dkv_even, dkv_odd = attention(
        me.reshape(1), query_segs, key_segs, queries, grad_attn, kv_even, kv_odd, kv_here, per_kv
    )
    if special:
        input_grad, dkv_mine = paired(dq, dkv_even, dkv_odd, quarters, me, col)
    else:
        dq = dq.reshape(kv_here, 2, rows, -1).transpose(2, 0, 1, 3).reshape(rows, heads_here * HD)
        input_grad = jnp.dot(
            lax.all_gather(dq, "col", axis=1, tiled=True),
            lax.all_gather(q_weight, "row", axis=0, tiled=True),
            preferred_element_type=jnp.float32,
        ).astype(jnp.bfloat16)
        dkv_mine = chips_sum(added(dkv_even, across(dkv_odd, 1)))

    share = max(1, group // heads_here)
    if share == 1:
        key_grad, value_grad = by_column(
            col.reshape(1), [dkv_mine] + [turned(dkv_mine, k) for k in range(1, count)]
        )
        return (input_grad, key_grad, value_grad)
    whole = lax.all_gather(dkv_mine, "col")
    whole = whole.reshape(count // share, share, rows, -1).astype(jnp.float32)
    whole = whole.sum(axis=1).astype(jnp.bfloat16)
    key_grad = jnp.concatenate(list(whole[:, :, :HD]), axis=1)
    value_grad = jnp.concatenate(list(whole[:, :, HD:]), axis=1)
    return (input_grad, key_grad, value_grad)


def chips_sum(terms):
    total = terms[0].astype(jnp.float32)
    for i in range(1, terms.shape[0]):
        total += across(terms[i], 2 * i).astype(jnp.float32)
    return total.astype(jnp.bfloat16)


def paired(dq, dkv_even, dkv_odd, quarters, me, col):
    count = lax.axis_size("col")
    rows = dq.shape[2]
    core = me & 1
    side = (me >> 1) & 1

    keep_one, keep_two, send_one, send_two = quarters
    w_one = across(send_one, 2)
    keep_one_y = across(keep_one, 4)

    mine = lax.dynamic_index_in_dim(dq, core, 0, keepdims=False)
    theirs = across(lax.dynamic_index_in_dim(dq, 1 - core, 0, keepdims=False), 1)
    both = jnp.stack([mine, theirs], axis=1)
    keep = lax.dynamic_index_in_dim(both, side, 0, keepdims=False)
    send = lax.dynamic_index_in_dim(both, 1 - side, 0, keepdims=False)
    send, w_one, keep_one_y = tied(send, w_one, keep_one_y)
    keep_two_y = across(keep_two, 4)
    step = rows // 2
    blocks = [jnp.concatenate([keep[:, :step], across(send[:, :step], 2)], axis=0)]
    send_two, blocks[0] = tied(send_two, blocks[0])
    near = [[turned(blocks[0], 1), turned(blocks[0], -1)]]
    w_two = across(send_two, 2)
    w_one_y = across(w_one, 4)
    send, w_two = tied(send, w_two)
    blocks.append(jnp.concatenate([keep[:, step:], across(send[:, step:], 2)], axis=0))
    keep_two_y, *near[0] = tied(keep_two_y, *near[0])
    far = [opposite(*near[0])]
    blocks[1], *near[0] = tied(blocks[1], *near[0])
    near.append([turned(blocks[1], 1), turned(blocks[1], -1)])
    w_two_y = across(w_two, 4)
    dkv_terms = added(dkv_even, across(dkv_odd, 1))
    dkv_mine = chips_sum(dkv_terms)
    w_one_y, dkv_mine, *near[1] = tied(w_one_y, dkv_mine, *near[1])
    far.append(opposite(*near[1]))

    def joined(*parts):
        return jnp.concatenate(parts, axis=0)

    weights = [
        joined(keep_one, keep_two), joined(w_one, w_two),
        joined(keep_one_y, keep_two_y), joined(w_one_y, w_two_y),
    ]
    slots = ((me >> 1) ^ ((col + jnp.arange(count)) % count)).astype(jnp.int32)
    outs = []
    for c in range(2):
        parts = [blocks[c], near[c][0], jnp.concatenate(far[c], axis=0), near[c][1]]
        even, odd = project(slots, weights, parts)
        half_sum = added(even, across(odd, 1))
        outs.append(added(half_sum[0], across(half_sum[1], 2)))
    return jnp.concatenate(outs, axis=0), dkv_mine


def solution(mesh):
    placed = (
        P("row", "col"),
        P("row", None),
        P("row", None),
        P("row", "col"),
        P(),
        P("row", "col"),
    )
    return jax.shard_map(
        local,
        mesh=mesh,
        in_specs=placed,
        out_specs=(P("row", "col"), P("row", None), P("row", None)),
        check_vma=False,
    )
```

```python
import functools
import math

import jax
import jax.numpy as jnp
from jax import lax
from jax.experimental import pallas as pl
from jax.experimental.pallas import tpu as pltpu
from jax.sharding import PartitionSpec as P

H = 64
KVH = 8
HD = 128

NEG = -1e30


def attention_kernel(
    per_kv, rows, ranks, me_ref, seg_query, seg_key, q_ref, g_ref, kv_even, kv_odd,
    dq_ref, dkv_even, dkv_odd, q_rows, g_rows, q_cols, g_cols, s_all, d_all, p_low, d_low, top, total, dots,
):
    half = rows // 2
    inv_root = 1.0 / math.sqrt(HD)
    scale = inv_root * math.log2(math.e)
    me = me_ref[0]
    parity = me & 1
    contract_last = (((1,), (1,)), ((), ()))
    dkv_even[...] = jnp.zeros_like(dkv_even)
    dkv_odd[...] = jnp.zeros_like(dkv_odd)
    for side in range(2):
        here = slice(side * half, (side + 1) * half)
        blocks = me + 1 if side == 0 else ranks - me
        steps = (blocks + 1) // 2
        swap = parity if side == 0 else 1 - parity
        for p in range(per_kv):
            head = slice(p * HD, (p + 1) * HD)
            q_rows[p * half:(p + 1) * half, :] = q_ref[here, head]
            g_rows[p * half:(p + 1) * half, :] = g_ref[here, head]
        q_cols[...] = q_rows[...].T
        g_cols[...] = g_rows[...].T

        def slot(j):
            chip = j if side == 0 else ranks // 2 - 1 - j
            return chip ^ (me >> 1)

        def pair(j, first):
            at = slot(j)
            cols = slice(first, first + HD)
            return jnp.concatenate([kv_even[at, here, cols], kv_odd[at, here, cols]], axis=0)

        top[...] = jnp.full_like(top, NEG)
        total[...] = jnp.zeros_like(total)
        dots[...] = jnp.zeros_like(dots)

        def scores(j, carry):
            keys = pair(j, 0)
            vals = pair(j, HD)
            query_at = (blocks - 1) * half + lax.broadcasted_iota(jnp.int32, (half, half), 0)
            bias = []
            for block in (2 * j + swap, 2 * j + 1 - swap):
                key_at = block * half + lax.broadcasted_iota(jnp.int32, (half, half), 1)
                segs = seg_key[side * ranks + block]
                allowed = (key_at <= query_at) & (segs == seg_query[side])
                bias.append(jnp.where(allowed, 0.0, NEG))
            bias = jnp.concatenate(bias, axis=1)
            for p in range(per_kv):
                at = slice(p * half, (p + 1) * half)
                s = lax.dot_general(
                    q_rows[at, :], keys, contract_last, preferred_element_type=jnp.float32
                )
                s = s * scale + bias
                s_all[j, at, :] = s
                d = lax.dot_general(
                    g_rows[at, :], vals, contract_last, preferred_element_type=jnp.float32
                )
                d_all[j, at, :] = d
                old = top[at, :]
                new = jnp.maximum(old, jnp.maximum(s[:, :half], s[:, half:]))
                factor = jnp.exp2(old - new)
                one = jnp.exp2(s[:, :half] - new)
                two = jnp.exp2(s[:, half:] - new)
                top[at, :] = new
                total[at, :] = total[at, :] * factor + (one + two)
                dots[at, :] = dots[at, :] * factor + (one * d[:, :half] + two * d[:, half:])
            return carry

        lax.fori_loop(0, steps, scores, 0)
        lanes = top[...]
        high = jnp.max(lanes, axis=1, keepdims=True)
        factor = jnp.exp2(lanes - high)
        sums = jnp.sum(total[...] * factor, axis=1, keepdims=True)
        delta = jnp.sum(dots[...] * factor, axis=1, keepdims=True) / sums
        total[...] = jnp.broadcast_to(high + jnp.log2(sums), total.shape)
        dots[...] = jnp.broadcast_to(delta, dots.shape)
        top[...] = jnp.zeros_like(top)

        def grads(j, carry):
            keys = pair(j, 0)
            for p in range(per_kv):
                at = slice(p * half, (p + 1) * half)
                lse = total[at, :]
                dot = dots[at, :]
                prob = jnp.exp2(s_all[j, at, :] - jnp.concatenate([lse, lse], axis=1))
                p_low[at, :] = prob.astype(jnp.bfloat16)
                shifted = d_all[j, at, :] - jnp.concatenate([dot, dot], axis=1)
                d_low[at, :] = (prob * shifted).astype(jnp.bfloat16)
            top[...] += jnp.dot(d_low[...], keys, preferred_element_type=jnp.float32)
            key_part = jnp.dot(q_cols[...], d_low[...], preferred_element_type=jnp.float32)
            val_part = jnp.dot(g_cols[...], p_low[...], preferred_element_type=jnp.float32)
            key_part = (key_part * inv_root).T.astype(jnp.bfloat16)
            val_part = val_part.T.astype(jnp.bfloat16)
            at = slot(j)
            dkv_even[at, here, :HD] = key_part[:half, :]
            dkv_odd[at, here, :HD] = key_part[half:, :]
            dkv_even[at, here, HD:] = val_part[:half, :]
            dkv_odd[at, here, HD:] = val_part[half:, :]
            return carry

        lax.fori_loop(0, steps, grads, 0)
        grad = (top[...] * inv_root).astype(jnp.bfloat16)
        for p in range(per_kv):
            part, at = divmod(p, per_kv // 2)
            dq_ref[0, part, here, at * HD:(at + 1) * HD] = grad[p * half:(p + 1) * half, :]


def attention(me, seg_query, seg_key, queries, grad_attn, kv_even, kv_odd, kv_here, per_kv):
    pairs, rows, width = kv_even.shape
    ranks = 2 * pairs
    half = rows // 2
    stack = per_kv * half
    vmem = pl.BlockSpec(memory_space=pltpu.VMEM)
    heads = pl.BlockSpec((rows, per_kv * HD), lambda g: (0, g))
    kv_spec = pl.BlockSpec((pairs, rows, 2 * HD), lambda g: (0, 0, g))
    wide = per_kv // 2 * HD
    return pl.pallas_call(
        functools.partial(attention_kernel, per_kv, rows, ranks),
        out_shape=[jax.ShapeDtypeStruct((kv_here, 2, rows, wide), jnp.bfloat16)]
        + [jax.ShapeDtypeStruct((pairs, rows, width), jnp.bfloat16)] * 2,
        grid=(kv_here,),
        in_specs=[pl.BlockSpec(memory_space=pltpu.SMEM), vmem, vmem, heads, heads, kv_spec, kv_spec],
        out_specs=[pl.BlockSpec((1, 2, rows, wide), lambda g: (g, 0, 0, 0)), kv_spec, kv_spec],
        scratch_shapes=[
            pltpu.VMEM((stack, HD), jnp.bfloat16),
            pltpu.VMEM((stack, HD), jnp.bfloat16),
            pltpu.VMEM((HD, stack), jnp.bfloat16),
            pltpu.VMEM((HD, stack), jnp.bfloat16),
            pltpu.VMEM((pairs, stack, 2 * half), jnp.float32),
            pltpu.VMEM((pairs, stack, 2 * half), jnp.float32),
            pltpu.VMEM((stack, 2 * half), jnp.bfloat16),
            pltpu.VMEM((stack, 2 * half), jnp.bfloat16),
            pltpu.VMEM((stack, HD), jnp.float32),
            pltpu.VMEM((stack, HD), jnp.float32),
            pltpu.VMEM((stack, HD), jnp.float32),
        ],
        compiler_params=pltpu.CompilerParams(vmem_limit_bytes=32 << 20),
        cost_estimate=pl.CostEstimate(
            flops=3_400_000_000, bytes_accessed=8_000_000, transcendentals=2_600_000
        ),
        name="attention",
    )(me, seg_query, seg_key, queries, grad_attn, kv_even, kv_odd)


def project_kernel(pieces_here, places, slot_ref, *refs):
    group = len(places[0])
    count = len(places)
    outs, lhs = refs[-1 - group:-1], refs[-1]
    pieces, sources = refs[:pieces_here], refs[pieces_here:-1 - group]
    step, features = outs[0].shape
    depth = sources[0].shape[1]
    for k in range(count):
        at = pl.ds(pl.multiple_of(slot_ref[k] * depth, depth), depth)
        for i in range(group):
            source, first = places[k][i]
            lhs[i * step:(i + 1) * step, at] = sources[source][first:first + step, :]
    tile = min(256, features)

    def columns(n, carry):
        at = pl.ds(pl.multiple_of(n * tile, tile), tile)
        weight = jnp.concatenate([piece[:, at] for piece in pieces], axis=0)
        for i in range(group):
            rows = slice(i * step, (i + 1) * step)
            out = jnp.dot(lhs[rows, :], weight, preferred_element_type=jnp.float32)
            outs[i][:, at] = out.astype(jnp.bfloat16)
        return carry

    lax.fori_loop(0, features // tile, columns, 0)


def project(slots, weights, sources, places, step):
    count = len(weights)
    group = len(places[0])
    depth = sources[0].shape[1]
    pieces = [piece for weight in weights for piece in weight]
    features = pieces[0].shape[1]
    smem = pl.BlockSpec(memory_space=pltpu.SMEM)
    vmem = pl.BlockSpec(memory_space=pltpu.VMEM)
    return pl.pallas_call(
        functools.partial(project_kernel, len(pieces), places),
        out_shape=[jax.ShapeDtypeStruct((step, features), jnp.bfloat16)] * group,
        in_specs=[smem] + [vmem] * (len(pieces) + len(sources)),
        out_specs=[vmem] * group,
        scratch_shapes=[pltpu.VMEM((group * step, count * depth), jnp.bfloat16)],
        compiler_params=pltpu.CompilerParams(vmem_limit_bytes=32 << 20),
        cost_estimate=pl.CostEstimate(
            flops=2 * group * step * depth * count * features,
            bytes_accessed=2 * (group * step * features + count * depth * features),
            transcendentals=0,
        ),
        name="project",
    )(slots, *pieces, *sources)


def columns_kernel(col_ref, *refs):
    parts, outs = refs[:-2], refs[-2:]
    count = len(parts)
    heads = parts[0].shape[1] // (2 * HD)
    for k in range(count):
        where = lax.rem(col_ref[0] + k, count) * heads
        for i in range(2 * heads):
            at = pl.ds(pl.multiple_of((where + i // 2) * HD, HD), HD)
            outs[i % 2][:, at] = parts[k][:, i * HD:(i + 1) * HD]


def by_column(col, parts):
    rows, width = parts[0].shape
    vmem = pl.BlockSpec(memory_space=pltpu.VMEM)
    return pl.pallas_call(
        columns_kernel,
        out_shape=[jax.ShapeDtypeStruct((rows, len(parts) * width // 2), jnp.bfloat16)] * 2,
        in_specs=[pl.BlockSpec(memory_space=pltpu.SMEM)] + [vmem] * len(parts),
        out_specs=[vmem, vmem],
        name="by_column",
    )(col, *parts)


def across(block, mask):
    ranks = lax.axis_size("row")
    return lax.ppermute(block, "row", [(i, i ^ mask) for i in range(ranks)])


def turned(block, distance):
    count = lax.axis_size("col")
    return lax.ppermute(block, "col", [((i + distance) % count, i) for i in range(count)])


def opposite(ahead, behind):
    cut = ahead.shape[0] // 2
    return turned(ahead[:cut], 1), turned(behind[cut:], -1)


def added(one, two):
    return (one.astype(jnp.float32) + two.astype(jnp.float32)).astype(jnp.bfloat16)


def tied(*arrays):
    return lax.optimization_barrier(arrays)


def local(queries, keys, values, grad_attn, segment_ids, q_weight):
    rows = queries.shape[0]
    half = rows // 2
    ranks = lax.axis_size("row")
    count = lax.axis_size("col")
    heads_here = queries.shape[1] // HD
    group = H // KVH
    kv_here = max(1, heads_here // group)
    per_kv = heads_here // kv_here
    me = lax.axis_index("row")
    col = lax.axis_index("col")
    kv_first = col * heads_here // group

    mine = []
    for g in range(kv_here):
        for array in (keys, values):
            mine.append(lax.dynamic_slice_in_dim(array, (kv_first + g) * HD, HD, 1))
    mine = jnp.concatenate(mine, axis=1)
    kv_even = jnp.stack([mine] + [across(mine, d) for d in range(2, ranks, 2)])
    rows_w = q_weight.shape[0]
    special = ranks == 8 and count == 4
    if special:
        side = (me >> 1) & 1
        wide = rows_w // 2
        pieces = []
        for start, size in (
            (side * wide, wide // 2), (side * wide + wide // 2, wide // 2),
            ((1 - side) * wide, wide // 2), ((1 - side) * wide + wide // 2, wide // 2),
        ):
            pieces.append(lax.dynamic_slice_in_dim(q_weight, start, size, 0))
        kv_even, *pieces = tied(kv_even, *pieces)
    kv_odd = across(kv_even, 1)

    key_segs = segment_ids.reshape(2 * ranks, 1, half)
    own = segment_ids.reshape(2 * ranks, half)
    query_segs = jnp.stack(
        [
            lax.dynamic_index_in_dim(own, me, 0, keepdims=False),
            lax.dynamic_index_in_dim(own, 2 * ranks - 1 - me, 0, keepdims=False),
        ]
    )[:, :, None]
    dq, dkv_even, dkv_odd = attention(
        me.reshape(1), query_segs, key_segs, queries, grad_attn, kv_even, kv_odd, kv_here, per_kv
    )
    if special:
        input_grad, dkv_mine = paired(dq, dkv_even, dkv_odd, pieces, me, col)
    else:
        dq = dq.reshape(kv_here, 2, rows, -1).transpose(2, 0, 1, 3).reshape(rows, heads_here * HD)
        input_grad = jnp.dot(
            lax.all_gather(dq, "col", axis=1, tiled=True),
            lax.all_gather(q_weight, "row", axis=0, tiled=True),
            preferred_element_type=jnp.float32,
        ).astype(jnp.bfloat16)
        dkv_mine = chips_sum(added(dkv_even, across(dkv_odd, 1)))

    share = max(1, group // heads_here)
    if share == 1:
        parts = dkv_mine if special else [dkv_mine] + [turned(dkv_mine, k) for k in range(1, count)]
        key_grad, value_grad = by_column(col.reshape(1), parts)
        return (input_grad, key_grad, value_grad)
    whole = lax.all_gather(dkv_mine, "col")
    whole = whole.reshape(count // share, share, rows, -1).astype(jnp.float32)
    whole = whole.sum(axis=1).astype(jnp.bfloat16)
    key_grad = jnp.concatenate(list(whole[:, :, :HD]), axis=1)
    value_grad = jnp.concatenate(list(whole[:, :, HD:]), axis=1)
    return (input_grad, key_grad, value_grad)


def chips_sum(terms):
    total = terms[0].astype(jnp.float32)
    for i in range(1, terms.shape[0]):
        total += across(terms[i], 2 * i).astype(jnp.float32)
    return total.astype(jnp.bfloat16)


def paired(dq, dkv_even, dkv_odd, pieces, me, col):
    count = lax.axis_size("col")
    rows = dq.shape[2]
    core = me & 1
    side = (me >> 1) & 1

    keep_w, (send_one, send_two) = pieces[:2], pieces[2:]

    def x(block):
        return across(block, 2)

    def y(block):
        return across(block, 4)

    w_one = x(send_one)
    keep_one_y = y(keep_w[0])

    mine = lax.dynamic_index_in_dim(dq, core, 0, keepdims=False)
    theirs = across(lax.dynamic_index_in_dim(dq, 1 - core, 0, keepdims=False), 1)
    both = jnp.stack([mine, theirs], axis=1)
    keep = lax.dynamic_index_in_dim(both, side, 0, keepdims=False)
    send = lax.dynamic_index_in_dim(both, 1 - side, 0, keepdims=False)
    send, w_one, keep_one_y = tied(send, w_one, keep_one_y)
    keep_two_y = y(keep_w[1])
    tokens = jnp.concatenate([keep, x(send)], axis=0)
    tokens = tokens.reshape(4 * rows, -1)
    send_two, tokens = tied(send_two, tokens)
    near = [turned(tokens, 1), turned(tokens, -1)]
    w_two = x(send_two)
    w_one_y = y(w_one)
    dkv_terms = added(dkv_even, across(dkv_odd, 1))
    dkv_terms, w_two = tied(dkv_terms, w_two)
    dkv_x = x(dkv_terms[1::2])
    w_two_y = y(w_two)
    keep_two_y, w_one_y, dkv_x, near[0], near[1] = tied(keep_two_y, w_one_y, dkv_x, *near)
    cut = 2 * rows
    far = [turned(near[0][:cut], 1), turned(near[1][cut:], -1)]
    dkv_terms = added(dkv_terms[0::2], dkv_x)
    dkv_y = y(dkv_terms[1])
    w_two_y, dkv_y = tied(w_two_y, dkv_y)

    weights = [keep_w, [w_one, w_two], [keep_one_y, keep_two_y], [w_one_y, w_two_y]]
    slots = ((me >> 1) ^ ((col + jnp.arange(count)) % count)).astype(jnp.int32)

    def partial(devices):
        places = [[(k, d * rows) for d in devices] for k in (0, 1)]
        places.append([(3 + d // 2, d % 2 * rows) for d in devices])
        places.append([(2, d * rows) for d in devices])
        return project(slots, weights, [tokens, *near, *far], places, rows)

    zero, one, two, three = partial(range(4))
    there = added(two, across(three, 1))
    found = across(one, 1)
    got = x(there)
    dkv_mine = added(dkv_terms[0], dkv_y)
    dkv_all = [dkv_mine] + [turned(dkv_mine, k) for k in range(1, count)]
    total = zero.astype(jnp.float32) + found.astype(jnp.float32) + got.astype(jnp.float32)
    return total.astype(jnp.bfloat16), dkv_all


def solution(mesh):
    placed = (
        P("row", "col"),
        P("row", None),
        P("row", None),
        P("row", "col"),
        P(),
        P("row", "col"),
    )
    return jax.shard_map(
        local,
        mesh=mesh,
        in_specs=placed,
        out_specs=(P("row", "col"), P("row", None), P("row", None)),
        check_vma=False,
    )
```

```python
import functools
import math

import jax
import jax.numpy as jnp
from jax import lax
from jax.experimental import pallas as pl
from jax.experimental.pallas import tpu as pltpu
from jax.sharding import PartitionSpec as P

H = 64
KVH = 8
HD = 128

NEG = -1e30


def attention_kernel(
    per_kv, rows, ranks, me_ref, seg_query, seg_key, q_ref, g_ref, kv_even, kv_odd,
    dq_ref, dkv_even, dkv_odd, q_rows, g_rows, q_cols, g_cols, s_all, d_all, p_low, d_low, top, total, dots,
):
    half = rows // 2
    inv_root = 1.0 / math.sqrt(HD)
    scale = inv_root * math.log2(math.e)
    me = me_ref[0]
    parity = me & 1
    contract_last = (((1,), (1,)), ((), ()))
    dkv_even[...] = jnp.zeros_like(dkv_even)
    dkv_odd[...] = jnp.zeros_like(dkv_odd)
    for side in range(2):
        here = slice(side * half, (side + 1) * half)
        blocks = me + 1 if side == 0 else ranks - me
        steps = (blocks + 1) // 2
        swap = parity if side == 0 else 1 - parity
        for p in range(per_kv):
            head = slice(p * HD, (p + 1) * HD)
            q_rows[p * half:(p + 1) * half, :] = q_ref[here, head]
            g_rows[p * half:(p + 1) * half, :] = g_ref[here, head]
        q_cols[...] = q_rows[...].T
        g_cols[...] = g_rows[...].T

        def slot(j):
            chip = j if side == 0 else ranks // 2 - 1 - j
            return chip ^ (me >> 1)

        def pair(j, first):
            at = slot(j)
            cols = slice(first, first + HD)
            return jnp.concatenate([kv_even[at, here, cols], kv_odd[at, here, cols]], axis=0)

        top[...] = jnp.full_like(top, NEG)
        total[...] = jnp.zeros_like(total)
        dots[...] = jnp.zeros_like(dots)

        def scores(j, carry):
            keys = pair(j, 0)
            vals = pair(j, HD)
            query_at = (blocks - 1) * half + lax.broadcasted_iota(jnp.int32, (half, half), 0)
            bias = []
            for block in (2 * j + swap, 2 * j + 1 - swap):
                key_at = block * half + lax.broadcasted_iota(jnp.int32, (half, half), 1)
                segs = seg_key[side * ranks + block]
                allowed = (key_at <= query_at) & (segs == seg_query[side])
                bias.append(jnp.where(allowed, 0.0, NEG))
            bias = jnp.concatenate(bias, axis=1)
            for p in range(per_kv):
                at = slice(p * half, (p + 1) * half)
                s = lax.dot_general(
                    q_rows[at, :], keys, contract_last, preferred_element_type=jnp.float32
                )
                s = s * scale + bias
                s_all[j, at, :] = s
                d = lax.dot_general(
                    g_rows[at, :], vals, contract_last, preferred_element_type=jnp.float32
                )
                d_all[j, at, :] = d
                old = top[at, :]
                new = jnp.maximum(old, jnp.maximum(s[:, :half], s[:, half:]))
                factor = jnp.exp2(old - new)
                one = jnp.exp2(s[:, :half] - new)
                two = jnp.exp2(s[:, half:] - new)
                top[at, :] = new
                total[at, :] = total[at, :] * factor + (one + two)
                dots[at, :] = dots[at, :] * factor + (one * d[:, :half] + two * d[:, half:])
            return carry

        lax.fori_loop(0, steps, scores, 0)
        lanes = top[...]
        high = jnp.max(lanes, axis=1, keepdims=True)
        factor = jnp.exp2(lanes - high)
        sums = jnp.sum(total[...] * factor, axis=1, keepdims=True)
        delta = jnp.sum(dots[...] * factor, axis=1, keepdims=True) / sums
        total[...] = jnp.broadcast_to(high + jnp.log2(sums), total.shape)
        dots[...] = jnp.broadcast_to(delta, dots.shape)
        top[...] = jnp.zeros_like(top)

        def grads(j, carry):
            keys = pair(j, 0)
            for p in range(per_kv):
                at = slice(p * half, (p + 1) * half)
                lse = total[at, :]
                dot = dots[at, :]
                prob = jnp.exp2(s_all[j, at, :] - jnp.concatenate([lse, lse], axis=1))
                p_low[at, :] = prob.astype(jnp.bfloat16)
                shifted = d_all[j, at, :] - jnp.concatenate([dot, dot], axis=1)
                d_low[at, :] = (prob * shifted).astype(jnp.bfloat16)
            top[...] += jnp.dot(d_low[...], keys, preferred_element_type=jnp.float32)
            key_part = jnp.dot(q_cols[...], d_low[...], preferred_element_type=jnp.float32)
            val_part = jnp.dot(g_cols[...], p_low[...], preferred_element_type=jnp.float32)
            key_part = (key_part * inv_root).T.astype(jnp.bfloat16)
            val_part = val_part.T.astype(jnp.bfloat16)
            at = slot(j)
            dkv_even[at, here, :HD] = key_part[:half, :]
            dkv_odd[at, here, :HD] = key_part[half:, :]
            dkv_even[at, here, HD:] = val_part[:half, :]
            dkv_odd[at, here, HD:] = val_part[half:, :]
            return carry

        lax.fori_loop(0, steps, grads, 0)
        grad = (top[...] * inv_root).astype(jnp.bfloat16)
        for p in range(per_kv):
            part, at = divmod(p, per_kv // 2)
            dq_ref[0, part, here, at * HD:(at + 1) * HD] = grad[p * half:(p + 1) * half, :]


def attention(me, seg_query, seg_key, queries, grad_attn, kv_even, kv_odd, kv_here, per_kv):
    pairs, rows, width = kv_even.shape
    ranks = 2 * pairs
    half = rows // 2
    stack = per_kv * half
    vmem = pl.BlockSpec(memory_space=pltpu.VMEM)
    heads = pl.BlockSpec((rows, per_kv * HD), lambda g: (0, g))
    kv_spec = pl.BlockSpec((pairs, rows, 2 * HD), lambda g: (0, 0, g))
    wide = per_kv // 2 * HD
    return pl.pallas_call(
        functools.partial(attention_kernel, per_kv, rows, ranks),
        out_shape=[jax.ShapeDtypeStruct((kv_here, 2, rows, wide), jnp.bfloat16)]
        + [jax.ShapeDtypeStruct((pairs, rows, width), jnp.bfloat16)] * 2,
        grid=(kv_here,),
        in_specs=[pl.BlockSpec(memory_space=pltpu.SMEM), vmem, vmem, heads, heads, kv_spec, kv_spec],
        out_specs=[pl.BlockSpec((1, 2, rows, wide), lambda g: (g, 0, 0, 0)), kv_spec, kv_spec],
        scratch_shapes=[
            pltpu.VMEM((stack, HD), jnp.bfloat16),
            pltpu.VMEM((stack, HD), jnp.bfloat16),
            pltpu.VMEM((HD, stack), jnp.bfloat16),
            pltpu.VMEM((HD, stack), jnp.bfloat16),
            pltpu.VMEM((pairs, stack, 2 * half), jnp.float32),
            pltpu.VMEM((pairs, stack, 2 * half), jnp.float32),
            pltpu.VMEM((stack, 2 * half), jnp.bfloat16),
            pltpu.VMEM((stack, 2 * half), jnp.bfloat16),
            pltpu.VMEM((stack, HD), jnp.float32),
            pltpu.VMEM((stack, HD), jnp.float32),
            pltpu.VMEM((stack, HD), jnp.float32),
        ],
        compiler_params=pltpu.CompilerParams(vmem_limit_bytes=32 << 20),
        cost_estimate=pl.CostEstimate(
            flops=3_400_000_000, bytes_accessed=8_000_000, transcendentals=2_600_000
        ),
        name="attention",
    )(me, seg_query, seg_key, queries, grad_attn, kv_even, kv_odd)


def project_kernel(pieces_here, weights, places, rest, last_ref, slot_ref, *refs):
    group = len(places[0])
    outs, lhs = refs[-1 - group:-1], refs[-1]
    pieces, sources = refs[:pieces_here], refs[pieces_here:-1 - group]
    former = None
    if rest:
        sources, former = sources[:-group], sources[-group:]
    step, features = outs[0].shape
    depth = sources[0].shape[1]
    last = last_ref[0]
    for k, place in enumerate(places):
        slot = slot_ref[k]
        at = pl.multiple_of(0 if rest else jnp.where(slot > last, slot - 1, slot) * depth, depth)
        for i in range(group):
            source, first = place[i]
            lhs[i * step:(i + 1) * step, pl.ds(at, depth)] = sources[source][first:first + step, :]
    tile = min(256, features)
    for e in range(len(weights)):
        used = weights[e] if rest else sum(weights[:e] + weights[e + 1:], [])

        @pl.when(last == e)
        def _(used=used):
            def columns(n, carry):
                at = pl.ds(pl.multiple_of(n * tile, tile), tile)
                weight = [pieces[i][first:first + size, at] for i, first, size in used]
                weight = jnp.concatenate(weight, axis=0)
                for i in range(group):
                    rows = slice(i * step, (i + 1) * step)
                    out = jnp.dot(lhs[rows, :], weight, preferred_element_type=jnp.float32)
                    if former is not None:
                        out += former[i][:, at].astype(jnp.float32)
                    outs[i][:, at] = out.astype(jnp.bfloat16)
                return carry

            lax.fori_loop(0, features // tile, columns, 0)


def project(last, slots, pieces, weights, sources, places, step, former=()):
    group = len(places[0])
    depth = sources[0].shape[1]
    features = pieces[0].shape[1]
    smem = pl.BlockSpec(memory_space=pltpu.SMEM)
    vmem = pl.BlockSpec(memory_space=pltpu.VMEM)
    operands = [*pieces, *sources, *former]
    return pl.pallas_call(
        functools.partial(project_kernel, len(pieces), weights, places, bool(former)),
        out_shape=[jax.ShapeDtypeStruct((step, features), jnp.bfloat16)] * group,
        in_specs=[smem, smem] + [vmem] * len(operands),
        out_specs=[vmem] * group,
        scratch_shapes=[pltpu.VMEM((group * step, len(places) * depth), jnp.bfloat16)],
        compiler_params=pltpu.CompilerParams(vmem_limit_bytes=32 << 20),
        cost_estimate=pl.CostEstimate(
            flops=2 * group * step * depth * len(places) * features,
            bytes_accessed=2 * (group * step * features + len(places) * depth * features),
            transcendentals=0,
        ),
        name="project",
    )(last, slots, *operands)


def columns_kernel(col_ref, *refs):
    parts, outs = refs[:-2], refs[-2:]
    count = len(parts)
    heads = parts[0].shape[1] // (2 * HD)
    for k in range(count):
        where = lax.rem(col_ref[0] + k, count) * heads
        for i in range(2 * heads):
            at = pl.ds(pl.multiple_of((where + i // 2) * HD, HD), HD)
            outs[i % 2][:, at] = parts[k][:, i * HD:(i + 1) * HD]


def by_column(col, parts):
    rows, width = parts[0].shape
    vmem = pl.BlockSpec(memory_space=pltpu.VMEM)
    return pl.pallas_call(
        columns_kernel,
        out_shape=[jax.ShapeDtypeStruct((rows, len(parts) * width // 2), jnp.bfloat16)] * 2,
        in_specs=[pl.BlockSpec(memory_space=pltpu.SMEM)] + [vmem] * len(parts),
        out_specs=[vmem, vmem],
        name="by_column",
    )(col, *parts)


def across(block, mask):
    ranks = lax.axis_size("row")
    return lax.ppermute(block, "row", [(i, i ^ mask) for i in range(ranks)])


def turned(block, distance):
    count = lax.axis_size("col")
    return lax.ppermute(block, "col", [((i + distance) % count, i) for i in range(count)])


def opposite(ahead, behind):
    cut = ahead.shape[0] // 2
    return turned(ahead[:cut], 1), turned(behind[cut:], -1)


def added(one, two):
    return (one.astype(jnp.float32) + two.astype(jnp.float32)).astype(jnp.bfloat16)


def tied(*arrays):
    return lax.optimization_barrier(arrays)


def local(queries, keys, values, grad_attn, segment_ids, q_weight):
    rows = queries.shape[0]
    half = rows // 2
    ranks = lax.axis_size("row")
    count = lax.axis_size("col")
    heads_here = queries.shape[1] // HD
    group = H // KVH
    kv_here = max(1, heads_here // group)
    per_kv = heads_here // kv_here
    me = lax.axis_index("row")
    col = lax.axis_index("col")
    kv_first = col * heads_here // group

    mine = []
    for g in range(kv_here):
        for array in (keys, values):
            mine.append(lax.dynamic_slice_in_dim(array, (kv_first + g) * HD, HD, 1))
    mine = jnp.concatenate(mine, axis=1)
    kv_even = jnp.stack([mine] + [across(mine, d) for d in range(2, ranks, 2)])
    rows_w = q_weight.shape[0]
    special = ranks == 8 and count == 4
    if special:
        side = (me >> 1) & 1
        wide = rows_w // 2
        pieces = []
        for start, size in (
            (side * wide, wide // 2), (side * wide + wide // 2, wide // 4),
            (side * wide + wide * 3 // 4, wide // 4),
            ((1 - side) * wide, wide // 2), ((1 - side) * wide + wide // 2, wide // 2),
        ):
            pieces.append(lax.dynamic_slice_in_dim(q_weight, start, size, 0))
        kv_even, *pieces = tied(kv_even, *pieces)
    kv_odd = across(kv_even, 1)

    key_segs = segment_ids.reshape(2 * ranks, 1, half)
    own = segment_ids.reshape(2 * ranks, half)
    query_segs = jnp.stack(
        [
            lax.dynamic_index_in_dim(own, me, 0, keepdims=False),
            lax.dynamic_index_in_dim(own, 2 * ranks - 1 - me, 0, keepdims=False),
        ]
    )[:, :, None]
    dq, dkv_even, dkv_odd = attention(
        me.reshape(1), query_segs, key_segs, queries, grad_attn, kv_even, kv_odd, kv_here, per_kv
    )
    if special:
        input_grad, dkv_mine = paired(dq, dkv_even, dkv_odd, pieces, me, col)
    else:
        dq = dq.reshape(kv_here, 2, rows, -1).transpose(2, 0, 1, 3).reshape(rows, heads_here * HD)
        input_grad = jnp.dot(
            lax.all_gather(dq, "col", axis=1, tiled=True),
            lax.all_gather(q_weight, "row", axis=0, tiled=True),
            preferred_element_type=jnp.float32,
        ).astype(jnp.bfloat16)
        dkv_mine = chips_sum(added(dkv_even, across(dkv_odd, 1)))

    share = max(1, group // heads_here)
    if share == 1:
        parts = dkv_mine if special else [dkv_mine] + [turned(dkv_mine, k) for k in range(1, count)]
        key_grad, value_grad = by_column(col.reshape(1), parts)
        return (input_grad, key_grad, value_grad)
    whole = lax.all_gather(dkv_mine, "col")
    whole = whole.reshape(count // share, share, rows, -1).astype(jnp.float32)
    whole = whole.sum(axis=1).astype(jnp.bfloat16)
    key_grad = jnp.concatenate(list(whole[:, :, :HD]), axis=1)
    value_grad = jnp.concatenate(list(whole[:, :, HD:]), axis=1)
    return (input_grad, key_grad, value_grad)


def chips_sum(terms):
    total = terms[0].astype(jnp.float32)
    for i in range(1, terms.shape[0]):
        total += across(terms[i], 2 * i).astype(jnp.float32)
    return total.astype(jnp.bfloat16)


def paired(dq, dkv_even, dkv_odd, pieces, me, col):
    count = lax.axis_size("col")
    rows = dq.shape[2]
    core = me & 1
    side = (me >> 1) & 1

    keep_w, (send_one, send_two) = pieces[:3], pieces[3:]

    def x(block):
        return across(block, 2)

    def y(block):
        return across(block, 4)

    w_one = x(send_one)
    keep_one_y = y(keep_w[0])

    mine = lax.dynamic_index_in_dim(dq, core, 0, keepdims=False)
    theirs = across(lax.dynamic_index_in_dim(dq, 1 - core, 0, keepdims=False), 1)
    both = jnp.stack([mine, theirs], axis=1)
    keep = lax.dynamic_index_in_dim(both, side, 0, keepdims=False)
    send = lax.dynamic_index_in_dim(both, 1 - side, 0, keepdims=False)
    send, w_one, keep_one_y = tied(send, w_one, keep_one_y)
    keep_w[1], send = tied(keep_w[1], send)
    keep_two_y = y(keep_w[1])
    tokens = jnp.concatenate([keep, x(send)], axis=0)
    tokens = tokens.reshape(4 * rows, -1)
    last_one = jnp.concatenate([keep_w[2], w_one], axis=0)
    dkv_terms = added(dkv_even, across(dkv_odd, 1))
    send_two, last_one, keep_two_y, dkv_terms, tokens = tied(
        send_two, last_one, keep_two_y, dkv_terms, tokens
    )
    near = [turned(tokens, 1), turned(tokens, -1)]
    last_one_y = y(last_one)
    w_two = x(send_two)
    dkv_x = x(dkv_terms[1::2])
    w_two_y = y(w_two)
    last_one_y, near[0], near[1] = tied(last_one_y, *near)
    cut = 2 * rows
    far = [turned(near[0][:cut], 1), turned(near[1][cut:], -1)]
    dkv_terms = added(dkv_terms[0::2], dkv_x)
    dkv_y = y(dkv_terms[1])

    pieces = [*keep_w, w_one, w_two, keep_one_y, keep_two_y, last_one_y, w_two_y]
    sizes = [piece.shape[0] for piece in pieces]
    last = sizes[2]
    weights = [
        [(i, 0, sizes[i]) for i in (0, 1, 2)], [(i, 0, sizes[i]) for i in (3, 4)],
        [(5, 0, sizes[5]), (6, 0, sizes[6]), (7, 0, last)], [(7, last, sizes[7] - last), (8, 0, sizes[8])],
    ]
    slots = ((me >> 1) ^ ((col + jnp.arange(count)) % count)).astype(jnp.int32)
    devices = range(4)
    places = [[(k, d * rows) for d in devices] for k in range(3)]
    most = project(slots[2:3], slots[jnp.array([0, 1, 3])], pieces, weights, [tokens, *near], places, rows)
    *most, dkv_y = tied(*most, dkv_y)
    places = [[(d // 2, d % 2 * rows) for d in devices]]
    zero, one, two, three = project(slots[2:3], slots[2:3], pieces, weights, far, places, rows, most)
    there = added(two, across(three, 1))
    found = across(one, 1)
    got = x(there)
    dkv_mine = added(dkv_terms[0], dkv_y)
    dkv_all = [dkv_mine] + [turned(dkv_mine, k) for k in range(1, count)]
    mine = added(zero, found)
    mine, *dkv_all = tied(mine, *dkv_all)
    return added(mine, got), dkv_all


def solution(mesh):
    placed = (
        P("row", "col"),
        P("row", None),
        P("row", None),
        P("row", "col"),
        P(),
        P("row", "col"),
    )
    return jax.shard_map(
        local,
        mesh=mesh,
        in_specs=placed,
        out_specs=(P("row", "col"), P("row", None), P("row", None)),
        check_vma=False,
    )
```

```python
import functools
import math

import jax
import jax.numpy as jnp
from jax import lax
from jax.experimental import pallas as pl
from jax.experimental.pallas import tpu as pltpu
from jax.sharding import PartitionSpec as P

H = 64
KVH = 8
HD = 128

NEG = -1e30


def attention_kernel(
    per_kv, rows, ranks, me_ref, seg_query, seg_key, q_ref, g_ref, kv_even, kv_odd,
    dq_ref, dkv_even, dkv_odd, q_rows, g_rows, q_cols, g_cols, s_all, d_all, p_low, d_low, top, total, dots,
):
    half = rows // 2
    inv_root = 1.0 / math.sqrt(HD)
    scale = inv_root * math.log2(math.e)
    me = me_ref[0]
    parity = me & 1
    contract_last = (((1,), (1,)), ((), ()))
    dkv_even[...] = jnp.zeros_like(dkv_even)
    dkv_odd[...] = jnp.zeros_like(dkv_odd)
    for side in range(2):
        here = slice(side * half, (side + 1) * half)
        blocks = me + 1 if side == 0 else ranks - me
        steps = (blocks + 1) // 2
        swap = parity if side == 0 else 1 - parity
        for p in range(per_kv):
            head = slice(p * HD, (p + 1) * HD)
            q_rows[p * half:(p + 1) * half, :] = q_ref[here, head]
            g_rows[p * half:(p + 1) * half, :] = g_ref[here, head]
        q_cols[...] = q_rows[...].T
        g_cols[...] = g_rows[...].T

        def slot(j):
            chip = j if side == 0 else ranks // 2 - 1 - j
            return chip ^ (me >> 1)

        def pair(j, first):
            at = slot(j)
            cols = slice(first, first + HD)
            return jnp.concatenate([kv_even[at, here, cols], kv_odd[at, here, cols]], axis=0)

        top[...] = jnp.full_like(top, NEG)
        total[...] = jnp.zeros_like(total)
        dots[...] = jnp.zeros_like(dots)

        def scores(j, carry):
            keys = pair(j, 0)
            vals = pair(j, HD)
            query_at = (blocks - 1) * half + lax.broadcasted_iota(jnp.int32, (half, half), 0)
            bias = []
            for block in (2 * j + swap, 2 * j + 1 - swap):
                key_at = block * half + lax.broadcasted_iota(jnp.int32, (half, half), 1)
                segs = seg_key[side * ranks + block]
                allowed = (key_at <= query_at) & (segs == seg_query[side])
                bias.append(jnp.where(allowed, 0.0, NEG))
            bias = jnp.concatenate(bias, axis=1)
            for p in range(per_kv):
                at = slice(p * half, (p + 1) * half)
                s = lax.dot_general(
                    q_rows[at, :], keys, contract_last, preferred_element_type=jnp.float32
                )
                s = s * scale + bias
                s_all[j, at, :] = s
                d = lax.dot_general(
                    g_rows[at, :], vals, contract_last, preferred_element_type=jnp.float32
                )
                d_all[j, at, :] = d
                old = top[at, :]
                new = jnp.maximum(old, jnp.maximum(s[:, :half], s[:, half:]))
                factor = jnp.exp2(old - new)
                one = jnp.exp2(s[:, :half] - new)
                two = jnp.exp2(s[:, half:] - new)
                top[at, :] = new
                total[at, :] = total[at, :] * factor + (one + two)
                dots[at, :] = dots[at, :] * factor + (one * d[:, :half] + two * d[:, half:])
            return carry

        lax.fori_loop(0, steps, scores, 0)
        lanes = top[...]
        high = jnp.max(lanes, axis=1, keepdims=True)
        factor = jnp.exp2(lanes - high)
        sums = jnp.sum(total[...] * factor, axis=1, keepdims=True)
        delta = jnp.sum(dots[...] * factor, axis=1, keepdims=True) / sums
        total[...] = jnp.broadcast_to(high + jnp.log2(sums), total.shape)
        dots[...] = jnp.broadcast_to(delta, dots.shape)
        top[...] = jnp.zeros_like(top)

        def grads(j, carry):
            keys = pair(j, 0)
            for p in range(per_kv):
                at = slice(p * half, (p + 1) * half)
                lse = total[at, :]
                dot = dots[at, :]
                prob = jnp.exp2(s_all[j, at, :] - jnp.concatenate([lse, lse], axis=1))
                p_low[at, :] = prob.astype(jnp.bfloat16)
                shifted = d_all[j, at, :] - jnp.concatenate([dot, dot], axis=1)
                d_low[at, :] = (prob * shifted).astype(jnp.bfloat16)
            top[...] += jnp.dot(d_low[...], keys, preferred_element_type=jnp.float32)
            key_part = jnp.dot(q_cols[...], d_low[...], preferred_element_type=jnp.float32)
            val_part = jnp.dot(g_cols[...], p_low[...], preferred_element_type=jnp.float32)
            key_part = (key_part * inv_root).T.astype(jnp.bfloat16)
            val_part = val_part.T.astype(jnp.bfloat16)
            at = slot(j)
            dkv_even[at, here, :HD] = key_part[:half, :]
            dkv_odd[at, here, :HD] = key_part[half:, :]
            dkv_even[at, here, HD:] = val_part[:half, :]
            dkv_odd[at, here, HD:] = val_part[half:, :]
            return carry

        lax.fori_loop(0, steps, grads, 0)
        grad = (top[...] * inv_root).astype(jnp.bfloat16)
        for p in range(per_kv):
            part, at = divmod(p, per_kv // 2)
            dq_ref[0, part, here, at * HD:(at + 1) * HD] = grad[p * half:(p + 1) * half, :]


def attention(me, seg_query, seg_key, queries, grad_attn, kv_even, kv_odd, kv_here, per_kv):
    pairs, rows, width = kv_even.shape
    ranks = 2 * pairs
    half = rows // 2
    stack = per_kv * half
    vmem = pl.BlockSpec(memory_space=pltpu.VMEM)
    heads = pl.BlockSpec((rows, per_kv * HD), lambda g: (0, g))
    kv_spec = pl.BlockSpec((pairs, rows, 2 * HD), lambda g: (0, 0, g))
    wide = per_kv // 2 * HD
    return pl.pallas_call(
        functools.partial(attention_kernel, per_kv, rows, ranks),
        out_shape=[jax.ShapeDtypeStruct((kv_here, 2, rows, wide), jnp.bfloat16)]
        + [jax.ShapeDtypeStruct((pairs, rows, width), jnp.bfloat16)] * 2,
        grid=(kv_here,),
        in_specs=[pl.BlockSpec(memory_space=pltpu.SMEM), vmem, vmem, heads, heads, kv_spec, kv_spec],
        out_specs=[pl.BlockSpec((1, 2, rows, wide), lambda g: (g, 0, 0, 0)), kv_spec, kv_spec],
        scratch_shapes=[
            pltpu.VMEM((stack, HD), jnp.bfloat16),
            pltpu.VMEM((stack, HD), jnp.bfloat16),
            pltpu.VMEM((HD, stack), jnp.bfloat16),
            pltpu.VMEM((HD, stack), jnp.bfloat16),
            pltpu.VMEM((pairs, stack, 2 * half), jnp.float32),
            pltpu.VMEM((pairs, stack, 2 * half), jnp.float32),
            pltpu.VMEM((stack, 2 * half), jnp.bfloat16),
            pltpu.VMEM((stack, 2 * half), jnp.bfloat16),
            pltpu.VMEM((stack, HD), jnp.float32),
            pltpu.VMEM((stack, HD), jnp.float32),
            pltpu.VMEM((stack, HD), jnp.float32),
        ],
        compiler_params=pltpu.CompilerParams(vmem_limit_bytes=32 << 20),
        cost_estimate=pl.CostEstimate(
            flops=3_400_000_000, bytes_accessed=8_000_000, transcendentals=2_600_000
        ),
        name="attention",
    )(me, seg_query, seg_key, queries, grad_attn, kv_even, kv_odd)


def gather_rows(places, sources, lhs, step, at):
    depth = sources[0].shape[1]
    for i, (source, first) in enumerate(places):
        lhs[i * step:(i + 1) * step, pl.ds(at, depth)] = sources[source][first:first + step, :]


def most_kernel(pieces_here, weights, places, last_ref, slot_ref, *refs):
    group = len(places[0])
    outs, last_out, lhs = refs[-2 - group:-2], refs[-2], refs[-1]
    pieces, sources = refs[:pieces_here], refs[pieces_here:-2 - group]
    step, features = outs[0].shape
    depth = sources[0].shape[1]
    last = last_ref[0]
    for k, place in enumerate(places):
        slot = slot_ref[k]
        at = pl.multiple_of(jnp.where(slot > last, slot - 1, slot) * depth, depth)
        gather_rows(place, sources, lhs, step, at)
    tile = min(256, features)

    def joined(used, at):
        return jnp.concatenate([pieces[i][first:first + size, at] for i, first, size in used], axis=0)

    for e in range(len(weights)):
        used = sum(weights[:e] + weights[e + 1:], [])

        @pl.when(last == e)
        def _(e=e, used=used):
            def columns(n, carry):
                at = pl.ds(pl.multiple_of(n * tile, tile), tile)
                last_out[:, at] = joined(weights[e], at)
                weight = joined(used, at)
                for i in range(group):
                    rows = slice(i * step, (i + 1) * step)
                    out = jnp.dot(lhs[rows, :], weight, preferred_element_type=jnp.float32)
                    outs[i][:, at] = out.astype(jnp.bfloat16)
                return carry

            lax.fori_loop(0, features // tile, columns, 0)


def rest_kernel(places, weight_ref, *refs):
    group = len(places)
    outs, lhs = refs[-1 - group:-1], refs[-1]
    sources, former = refs[:-1 - 2 * group], refs[-1 - 2 * group:-1 - group]
    step, features = outs[0].shape
    gather_rows(places, sources, lhs, step, 0)
    tile = min(256, features)

    def columns(n, carry):
        at = pl.ds(pl.multiple_of(n * tile, tile), tile)
        weight = weight_ref[:, at]
        for i in range(group):
            rows = slice(i * step, (i + 1) * step)
            out = jnp.dot(lhs[rows, :], weight, preferred_element_type=jnp.float32)
            outs[i][:, at] = (out + former[i][:, at].astype(jnp.float32)).astype(jnp.bfloat16)
        return carry

    lax.fori_loop(0, features // tile, columns, 0)


def project(last, slots, pieces, weights, sources, places, step):
    group = len(places[0])
    depth = sources[0].shape[1]
    features = pieces[0].shape[1]
    smem = pl.BlockSpec(memory_space=pltpu.SMEM)
    vmem = pl.BlockSpec(memory_space=pltpu.VMEM)
    operands = [*pieces, *sources]
    return pl.pallas_call(
        functools.partial(most_kernel, len(pieces), weights, places),
        out_shape=[jax.ShapeDtypeStruct((step, features), jnp.bfloat16)] * group
        + [jax.ShapeDtypeStruct((depth, features), jnp.bfloat16)],
        in_specs=[smem, smem] + [vmem] * len(operands),
        out_specs=[vmem] * (group + 1),
        scratch_shapes=[pltpu.VMEM((group * step, len(places) * depth), jnp.bfloat16)],
        compiler_params=pltpu.CompilerParams(vmem_limit_bytes=32 << 20),
        cost_estimate=pl.CostEstimate(
            flops=2 * group * step * depth * len(places) * features,
            bytes_accessed=2 * (group * step * features + len(places) * depth * features),
            transcendentals=0,
        ),
        name="project_most",
    )(last, slots, *operands)


def project_rest(weight, sources, places, step, former):
    depth, features = weight.shape
    group = len(places)
    vmem = pl.BlockSpec(memory_space=pltpu.VMEM)
    operands = [*sources, *former]
    return pl.pallas_call(
        functools.partial(rest_kernel, places),
        out_shape=[jax.ShapeDtypeStruct((step, features), jnp.bfloat16)] * group,
        in_specs=[vmem] * (1 + len(operands)),
        out_specs=[vmem] * group,
        scratch_shapes=[pltpu.VMEM((group * step, depth), jnp.bfloat16)],
        compiler_params=pltpu.CompilerParams(vmem_limit_bytes=32 << 20),
        cost_estimate=pl.CostEstimate(
            flops=2 * group * step * depth * features,
            bytes_accessed=2 * (2 * group * step * features + depth * features),
            transcendentals=0,
        ),
        name="project_rest",
    )(weight, *operands)


def columns_kernel(col_ref, *refs):
    parts, outs = refs[:-2], refs[-2:]
    count = len(parts)
    heads = parts[0].shape[1] // (2 * HD)
    for k in range(count):
        where = lax.rem(col_ref[0] + k, count) * heads
        for i in range(2 * heads):
            at = pl.ds(pl.multiple_of((where + i // 2) * HD, HD), HD)
            outs[i % 2][:, at] = parts[k][:, i * HD:(i + 1) * HD]


def by_column(col, parts):
    rows, width = parts[0].shape
    vmem = pl.BlockSpec(memory_space=pltpu.VMEM)
    return pl.pallas_call(
        columns_kernel,
        out_shape=[jax.ShapeDtypeStruct((rows, len(parts) * width // 2), jnp.bfloat16)] * 2,
        in_specs=[pl.BlockSpec(memory_space=pltpu.SMEM)] + [vmem] * len(parts),
        out_specs=[vmem, vmem],
        name="by_column",
    )(col, *parts)


def across(block, mask):
    ranks = lax.axis_size("row")
    return lax.ppermute(block, "row", [(i, i ^ mask) for i in range(ranks)])


def turned(block, distance):
    count = lax.axis_size("col")
    return lax.ppermute(block, "col", [((i + distance) % count, i) for i in range(count)])


def opposite(ahead, behind):
    cut = ahead.shape[0] // 2
    return turned(ahead[:cut], 1), turned(behind[cut:], -1)


def added(one, two):
    return (one.astype(jnp.float32) + two.astype(jnp.float32)).astype(jnp.bfloat16)


def tied(*arrays):
    return lax.optimization_barrier(arrays)


def local(queries, keys, values, grad_attn, segment_ids, q_weight):
    rows = queries.shape[0]
    half = rows // 2
    ranks = lax.axis_size("row")
    count = lax.axis_size("col")
    heads_here = queries.shape[1] // HD
    group = H // KVH
    kv_here = max(1, heads_here // group)
    per_kv = heads_here // kv_here
    me = lax.axis_index("row")
    col = lax.axis_index("col")
    kv_first = col * heads_here // group

    mine = []
    for g in range(kv_here):
        for array in (keys, values):
            mine.append(lax.dynamic_slice_in_dim(array, (kv_first + g) * HD, HD, 1))
    mine = jnp.concatenate(mine, axis=1)
    kv_even = jnp.stack([mine] + [across(mine, d) for d in range(2, ranks, 2)])
    rows_w = q_weight.shape[0]
    special = ranks == 8 and count == 4
    if special:
        side = (me >> 1) & 1
        wide = rows_w // 2
        pieces = []
        for start, size in (
            (side * wide, wide // 2), (side * wide + wide // 2, wide // 4),
            (side * wide + wide * 3 // 4, wide // 4),
            ((1 - side) * wide, wide // 2), ((1 - side) * wide + wide // 2, wide // 2),
        ):
            pieces.append(lax.dynamic_slice_in_dim(q_weight, start, size, 0))
        kv_even, *pieces = tied(kv_even, *pieces)
    kv_odd = across(kv_even, 1)

    key_segs = segment_ids.reshape(2 * ranks, 1, half)
    own = segment_ids.reshape(2 * ranks, half)
    query_segs = jnp.stack(
        [
            lax.dynamic_index_in_dim(own, me, 0, keepdims=False),
            lax.dynamic_index_in_dim(own, 2 * ranks - 1 - me, 0, keepdims=False),
        ]
    )[:, :, None]
    dq, dkv_even, dkv_odd = attention(
        me.reshape(1), query_segs, key_segs, queries, grad_attn, kv_even, kv_odd, kv_here, per_kv
    )
    if special:
        input_grad, dkv_mine = paired(dq, dkv_even, dkv_odd, pieces, me, col)
    else:
        dq = dq.reshape(kv_here, 2, rows, -1).transpose(2, 0, 1, 3).reshape(rows, heads_here * HD)
        input_grad = jnp.dot(
            lax.all_gather(dq, "col", axis=1, tiled=True),
            lax.all_gather(q_weight, "row", axis=0, tiled=True),
            preferred_element_type=jnp.float32,
        ).astype(jnp.bfloat16)
        dkv_mine = chips_sum(added(dkv_even, across(dkv_odd, 1)))

    share = max(1, group // heads_here)
    if share == 1:
        parts = dkv_mine if special else [dkv_mine] + [turned(dkv_mine, k) for k in range(1, count)]
        key_grad, value_grad = by_column(col.reshape(1), parts)
        return (input_grad, key_grad, value_grad)
    whole = lax.all_gather(dkv_mine, "col")
    whole = whole.reshape(count // share, share, rows, -1).astype(jnp.float32)
    whole = whole.sum(axis=1).astype(jnp.bfloat16)
    key_grad = jnp.concatenate(list(whole[:, :, :HD]), axis=1)
    value_grad = jnp.concatenate(list(whole[:, :, HD:]), axis=1)
    return (input_grad, key_grad, value_grad)


def chips_sum(terms):
    total = terms[0].astype(jnp.float32)
    for i in range(1, terms.shape[0]):
        total += across(terms[i], 2 * i).astype(jnp.float32)
    return total.astype(jnp.bfloat16)


def paired(dq, dkv_even, dkv_odd, pieces, me, col):
    count = lax.axis_size("col")
    rows = dq.shape[2]
    core = me & 1
    side = (me >> 1) & 1

    keep_w, (send_one, send_two) = pieces[:3], pieces[3:]

    def x(block):
        return across(block, 2)

    def y(block):
        return across(block, 4)

    w_one = x(send_one)
    keep_one_y = y(keep_w[0])

    mine = lax.dynamic_index_in_dim(dq, core, 0, keepdims=False)
    theirs = across(lax.dynamic_index_in_dim(dq, 1 - core, 0, keepdims=False), 1)
    both = jnp.stack([mine, theirs], axis=1)
    keep = lax.dynamic_index_in_dim(both, side, 0, keepdims=False)
    send = lax.dynamic_index_in_dim(both, 1 - side, 0, keepdims=False)
    send, w_one, keep_one_y = tied(send, w_one, keep_one_y)
    keep_w[1], send = tied(keep_w[1], send)
    keep_two_y = y(keep_w[1])
    tokens = jnp.concatenate([keep, x(send)], axis=0)
    tokens = tokens.reshape(4 * rows, -1)
    last_one = jnp.concatenate([keep_w[2], w_one], axis=0)
    dkv_terms = added(dkv_even, across(dkv_odd, 1))
    send_two, last_one, keep_two_y, dkv_terms, tokens = tied(
        send_two, last_one, keep_two_y, dkv_terms, tokens
    )
    near = [turned(tokens, 1), turned(tokens, -1)]
    last_one_y = y(last_one)
    w_two = x(send_two)
    dkv_x = x(dkv_terms[1::2])
    w_two_y = y(w_two)
    last_one_y, near[0], near[1] = tied(last_one_y, *near)
    cut = 2 * rows
    far = [turned(near[0][:cut], 1), turned(near[1][cut:], -1)]
    dkv_terms = added(dkv_terms[0::2], dkv_x)
    dkv_y = y(dkv_terms[1])

    pieces = [*keep_w, w_one, w_two, keep_one_y, keep_two_y, last_one_y, w_two_y]
    sizes = [piece.shape[0] for piece in pieces]
    last = sizes[2]
    weights = [
        [(i, 0, sizes[i]) for i in (0, 1, 2)], [(i, 0, sizes[i]) for i in (3, 4)],
        [(5, 0, sizes[5]), (6, 0, sizes[6]), (7, 0, last)], [(7, last, sizes[7] - last), (8, 0, sizes[8])],
    ]
    slots = ((me >> 1) ^ ((col + jnp.arange(count)) % count)).astype(jnp.int32)
    devices = range(4)
    places = [[(k, d * rows) for d in devices] for k in range(3)]
    *most, last_weight = project(slots[2:3], slots[jnp.array([0, 1, 3])], pieces, weights, [tokens, *near], places, rows)
    *most, dkv_y = tied(*most, dkv_y)
    places = [(d // 2, d % 2 * rows) for d in devices]
    zero, one, two, three = project_rest(last_weight, far, places, rows, most)
    there = added(two, across(three, 1))
    found = across(one, 1)
    got = x(there)
    dkv_mine = added(dkv_terms[0], dkv_y)
    dkv_all = [dkv_mine] + [turned(dkv_mine, k) for k in range(1, count)]
    mine = added(zero, found)
    mine, *dkv_all = tied(mine, *dkv_all)
    return added(mine, got), dkv_all


def solution(mesh):
    placed = (
        P("row", "col"),
        P("row", None),
        P("row", None),
        P("row", "col"),
        P(),
        P("row", "col"),
    )
    return jax.shard_map(
        local,
        mesh=mesh,
        in_specs=placed,
        out_specs=(P("row", "col"), P("row", None), P("row", None)),
        check_vma=False,
    )
```

```python
import functools
import math

import jax
import jax.numpy as jnp
from jax import lax
from jax.experimental import pallas as pl
from jax.experimental.pallas import tpu as pltpu
from jax.sharding import PartitionSpec as P

H = 64
KVH = 8
HD = 128

NEG = -1e30


def attention_kernel(
    per_kv, rows, ranks, me_ref, seg_query, seg_key, q_ref, g_ref, kv_even, kv_odd,
    dq_ref, dkv_even, dkv_odd, q_rows, g_rows, q_cols, g_cols, s_all, d_all, p_low, d_low, top, total, dots,
):
    half = rows // 2
    inv_root = 1.0 / math.sqrt(HD)
    scale = inv_root * math.log2(math.e)
    me = me_ref[0]
    parity = me & 1
    contract_last = (((1,), (1,)), ((), ()))
    dkv_even[...] = jnp.zeros_like(dkv_even)
    dkv_odd[...] = jnp.zeros_like(dkv_odd)
    for side in range(2):
        here = slice(side * half, (side + 1) * half)
        blocks = me + 1 if side == 0 else ranks - me
        steps = (blocks + 1) // 2
        swap = parity if side == 0 else 1 - parity
        for p in range(per_kv):
            head = slice(p * HD, (p + 1) * HD)
            q_rows[p * half:(p + 1) * half, :] = q_ref[here, head]
            g_rows[p * half:(p + 1) * half, :] = g_ref[here, head]
        q_cols[...] = q_rows[...].T
        g_cols[...] = g_rows[...].T

        def slot(j):
            chip = j if side == 0 else ranks // 2 - 1 - j
            return chip ^ (me >> 1)

        def pair(j, first):
            at = slot(j)
            cols = slice(first, first + HD)
            return jnp.concatenate([kv_even[at, here, cols], kv_odd[at, here, cols]], axis=0)

        top[...] = jnp.full_like(top, NEG)
        total[...] = jnp.zeros_like(total)
        dots[...] = jnp.zeros_like(dots)

        def scores(j, carry):
            keys = pair(j, 0)
            vals = pair(j, HD)
            query_at = (blocks - 1) * half + lax.broadcasted_iota(jnp.int32, (half, half), 0)
            bias = []
            for block in (2 * j + swap, 2 * j + 1 - swap):
                key_at = block * half + lax.broadcasted_iota(jnp.int32, (half, half), 1)
                segs = seg_key[side * ranks + block]
                allowed = (key_at <= query_at) & (segs == seg_query[side])
                bias.append(jnp.where(allowed, 0.0, NEG))
            bias = jnp.concatenate(bias, axis=1)
            for p in range(per_kv):
                at = slice(p * half, (p + 1) * half)
                s = lax.dot_general(
                    q_rows[at, :], keys, contract_last, preferred_element_type=jnp.float32
                )
                s = s * scale + bias
                s_all[j, at, :] = s
                d = lax.dot_general(
                    g_rows[at, :], vals, contract_last, preferred_element_type=jnp.float32
                )
                d_all[j, at, :] = d
                old = top[at, :]
                new = jnp.maximum(old, jnp.maximum(s[:, :half], s[:, half:]))
                factor = jnp.exp2(old - new)
                one = jnp.exp2(s[:, :half] - new)
                two = jnp.exp2(s[:, half:] - new)
                top[at, :] = new
                total[at, :] = total[at, :] * factor + (one + two)
                dots[at, :] = dots[at, :] * factor + (one * d[:, :half] + two * d[:, half:])
            return carry

        lax.fori_loop(0, steps, scores, 0)
        lanes = top[...]
        high = jnp.max(lanes, axis=1, keepdims=True)
        factor = jnp.exp2(lanes - high)
        sums = jnp.sum(total[...] * factor, axis=1, keepdims=True)
        delta = jnp.sum(dots[...] * factor, axis=1, keepdims=True) / sums
        total[...] = jnp.broadcast_to(high + jnp.log2(sums), total.shape)
        dots[...] = jnp.broadcast_to(delta, dots.shape)
        top[...] = jnp.zeros_like(top)

        def grads(j, carry):
            keys = pair(j, 0)
            for p in range(per_kv):
                at = slice(p * half, (p + 1) * half)
                lse = total[at, :]
                dot = dots[at, :]
                prob = jnp.exp2(s_all[j, at, :] - jnp.concatenate([lse, lse], axis=1))
                p_low[at, :] = prob.astype(jnp.bfloat16)
                shifted = d_all[j, at, :] - jnp.concatenate([dot, dot], axis=1)
                d_low[at, :] = (prob * shifted).astype(jnp.bfloat16)
            top[...] += jnp.dot(d_low[...], keys, preferred_element_type=jnp.float32)
            key_part = jnp.dot(q_cols[...], d_low[...], preferred_element_type=jnp.float32)
            val_part = jnp.dot(g_cols[...], p_low[...], preferred_element_type=jnp.float32)
            key_part = (key_part * inv_root).T.astype(jnp.bfloat16)
            val_part = val_part.T.astype(jnp.bfloat16)
            at = slot(j)
            dkv_even[at, here, :HD] = key_part[:half, :]
            dkv_odd[at, here, :HD] = key_part[half:, :]
            dkv_even[at, here, HD:] = val_part[:half, :]
            dkv_odd[at, here, HD:] = val_part[half:, :]
            return carry

        lax.fori_loop(0, steps, grads, 0)
        grad = (top[...] * inv_root).astype(jnp.bfloat16)
        for p in range(per_kv):
            part, at = divmod(p, per_kv // 2)
            dq_ref[0, part, here, at * HD:(at + 1) * HD] = grad[p * half:(p + 1) * half, :]


def attention(me, seg_query, seg_key, queries, grad_attn, kv_even, kv_odd, kv_here, per_kv):
    pairs, rows, width = kv_even.shape
    ranks = 2 * pairs
    half = rows // 2
    stack = per_kv * half
    vmem = pl.BlockSpec(memory_space=pltpu.VMEM)
    heads = pl.BlockSpec((rows, per_kv * HD), lambda g: (0, g))
    kv_spec = pl.BlockSpec((pairs, rows, 2 * HD), lambda g: (0, 0, g))
    wide = per_kv // 2 * HD
    return pl.pallas_call(
        functools.partial(attention_kernel, per_kv, rows, ranks),
        out_shape=[jax.ShapeDtypeStruct((kv_here, 2, rows, wide), jnp.bfloat16)]
        + [jax.ShapeDtypeStruct((pairs, rows, width), jnp.bfloat16)] * 2,
        grid=(kv_here,),
        in_specs=[pl.BlockSpec(memory_space=pltpu.SMEM), vmem, vmem, heads, heads, kv_spec, kv_spec],
        out_specs=[pl.BlockSpec((1, 2, rows, wide), lambda g: (g, 0, 0, 0)), kv_spec, kv_spec],
        scratch_shapes=[
            pltpu.VMEM((stack, HD), jnp.bfloat16),
            pltpu.VMEM((stack, HD), jnp.bfloat16),
            pltpu.VMEM((HD, stack), jnp.bfloat16),
            pltpu.VMEM((HD, stack), jnp.bfloat16),
            pltpu.VMEM((pairs, stack, 2 * half), jnp.float32),
            pltpu.VMEM((pairs, stack, 2 * half), jnp.float32),
            pltpu.VMEM((stack, 2 * half), jnp.bfloat16),
            pltpu.VMEM((stack, 2 * half), jnp.bfloat16),
            pltpu.VMEM((stack, HD), jnp.float32),
            pltpu.VMEM((stack, HD), jnp.float32),
            pltpu.VMEM((stack, HD), jnp.float32),
        ],
        compiler_params=pltpu.CompilerParams(vmem_limit_bytes=32 << 20),
        cost_estimate=pl.CostEstimate(
            flops=3_400_000_000, bytes_accessed=8_000_000, transcendentals=2_600_000
        ),
        name="attention",
    )(me, seg_query, seg_key, queries, grad_attn, kv_even, kv_odd)


def gather_rows(places, sources, lhs, step, at):
    depth = sources[0].shape[1]
    for i, (source, first) in enumerate(places):
        lhs[i * step:(i + 1) * step, pl.ds(at, depth)] = sources[source][first:first + step, :]


def most_kernel(pieces_here, weights, places, last_ref, slot_ref, *refs):
    group = len(places[0])
    outs, last_out, lhs = refs[-2 - group:-2], refs[-2], refs[-1]
    pieces, sources = refs[:pieces_here], refs[pieces_here:-2 - group]
    step, features = outs[0].shape
    depth = sources[0].shape[1]
    last = last_ref[0]
    for k, place in enumerate(places):
        slot = slot_ref[k]
        at = pl.multiple_of(jnp.where(slot > last, slot - 1, slot) * depth, depth)
        gather_rows(place, sources, lhs, step, at)
    tile = min(256, features)

    def joined(used, at):
        return jnp.concatenate([pieces[i][first:first + size, at] for i, first, size in used], axis=0)

    for e in range(len(weights)):
        used = sum(weights[:e] + weights[e + 1:], [])

        @pl.when(last == e)
        def _(e=e, used=used):
            def columns(n, carry):
                at = pl.ds(pl.multiple_of(n * tile, tile), tile)
                last_out[:, at] = joined(weights[e], at)
                weight = joined(used, at)
                for i in range(group):
                    rows = slice(i * step, (i + 1) * step)
                    out = jnp.dot(lhs[rows, :], weight, preferred_element_type=jnp.float32)
                    outs[i][:, at] = out.astype(jnp.bfloat16)
                return carry

            lax.fori_loop(0, features // tile, columns, 0)


def rest_kernel(places, weight_ref, *refs):
    group = len(places)
    outs, lhs = refs[-1 - group:-1], refs[-1]
    sources, former = refs[:-1 - 2 * group], refs[-1 - 2 * group:-1 - group]
    step, features = outs[0].shape
    gather_rows(places, sources, lhs, step, 0)
    tile = min(256, features)

    def columns(n, carry):
        at = pl.ds(pl.multiple_of(n * tile, tile), tile)
        weight = weight_ref[:, at]
        for i in range(group):
            rows = slice(i * step, (i + 1) * step)
            out = jnp.dot(lhs[rows, :], weight, preferred_element_type=jnp.float32)
            outs[i][:, at] = (out + former[i][:, at].astype(jnp.float32)).astype(jnp.bfloat16)
        return carry

    lax.fori_loop(0, features // tile, columns, 0)


def project(last, slots, pieces, weights, sources, places, step):
    group = len(places[0])
    depth = sources[0].shape[1]
    features = pieces[0].shape[1]
    smem = pl.BlockSpec(memory_space=pltpu.SMEM)
    vmem = pl.BlockSpec(memory_space=pltpu.VMEM)
    operands = [*pieces, *sources]
    return pl.pallas_call(
        functools.partial(most_kernel, len(pieces), weights, places),
        out_shape=[jax.ShapeDtypeStruct((step, features), jnp.bfloat16)] * group
        + [jax.ShapeDtypeStruct((depth, features), jnp.bfloat16)],
        in_specs=[smem, smem] + [vmem] * len(operands),
        out_specs=[vmem] * (group + 1),
        scratch_shapes=[pltpu.VMEM((group * step, len(places) * depth), jnp.bfloat16)],
        compiler_params=pltpu.CompilerParams(vmem_limit_bytes=32 << 20),
        cost_estimate=pl.CostEstimate(
            flops=2 * group * step * depth * len(places) * features,
            bytes_accessed=2 * (group * step * features + len(places) * depth * features),
            transcendentals=0,
        ),
        name="project_most",
    )(last, slots, *operands)


def project_rest(weight, sources, places, step, former):
    depth, features = weight.shape
    group = len(places)
    vmem = pl.BlockSpec(memory_space=pltpu.VMEM)
    operands = [*sources, *former]
    return pl.pallas_call(
        functools.partial(rest_kernel, places),
        out_shape=[jax.ShapeDtypeStruct((step, features), jnp.bfloat16)] * group,
        in_specs=[vmem] * (1 + len(operands)),
        out_specs=[vmem] * group,
        scratch_shapes=[pltpu.VMEM((group * step, depth), jnp.bfloat16)],
        compiler_params=pltpu.CompilerParams(vmem_limit_bytes=32 << 20),
        cost_estimate=pl.CostEstimate(
            flops=2 * group * step * depth * features,
            bytes_accessed=2 * (2 * group * step * features + depth * features),
            transcendentals=0,
        ),
        name="project_rest",
    )(weight, *operands)


def columns_kernel(col_ref, *refs):
    parts, outs = refs[:-2], refs[-2:]
    count = len(parts)
    heads = parts[0].shape[1] // (2 * HD)
    for k in range(count):
        where = lax.rem(col_ref[0] + k, count) * heads
        for i in range(2 * heads):
            at = pl.ds(pl.multiple_of((where + i // 2) * HD, HD), HD)
            outs[i % 2][:, at] = parts[k][:, i * HD:(i + 1) * HD]


def by_column(col, parts):
    rows, width = parts[0].shape
    vmem = pl.BlockSpec(memory_space=pltpu.VMEM)
    return pl.pallas_call(
        columns_kernel,
        out_shape=[jax.ShapeDtypeStruct((rows, len(parts) * width // 2), jnp.bfloat16)] * 2,
        in_specs=[pl.BlockSpec(memory_space=pltpu.SMEM)] + [vmem] * len(parts),
        out_specs=[vmem, vmem],
        name="by_column",
    )(col, *parts)


def across(block, mask):
    ranks = lax.axis_size("row")
    return lax.ppermute(block, "row", [(i, i ^ mask) for i in range(ranks)])


def turned(block, distance):
    count = lax.axis_size("col")
    return lax.ppermute(block, "col", [((i + distance) % count, i) for i in range(count)])


def opposite(ahead, behind):
    cut = ahead.shape[0] // 2
    return turned(ahead[:cut], 1), turned(behind[cut:], -1)


def added(one, two):
    return (one.astype(jnp.float32) + two.astype(jnp.float32)).astype(jnp.bfloat16)


def tied(*arrays):
    return lax.optimization_barrier(arrays)


def local(queries, keys, values, grad_attn, segment_ids, q_weight):
    rows = queries.shape[0]
    half = rows // 2
    ranks = lax.axis_size("row")
    count = lax.axis_size("col")
    heads_here = queries.shape[1] // HD
    group = H // KVH
    kv_here = max(1, heads_here // group)
    per_kv = heads_here // kv_here
    me = lax.axis_index("row")
    col = lax.axis_index("col")
    kv_first = col * heads_here // group

    mine = []
    for g in range(kv_here):
        for array in (keys, values):
            mine.append(lax.dynamic_slice_in_dim(array, (kv_first + g) * HD, HD, 1))
    mine = jnp.concatenate(mine, axis=1)
    kv_even = jnp.stack([mine] + [across(mine, d) for d in range(2, ranks, 2)])
    rows_w = q_weight.shape[0]
    special = ranks == 8 and count == 4
    if special:
        side = (me >> 1) & 1
        wide = rows_w // 2
        pieces = []
        for start, size in (
            (side * wide, wide // 2), (side * wide + wide // 2, wide // 2),
            ((1 - side) * wide, wide // 2), ((1 - side) * wide + wide // 2, wide // 2),
        ):
            pieces.append(lax.dynamic_slice_in_dim(q_weight, start, size, 0))
        kv_even, *pieces = tied(kv_even, *pieces)
    kv_odd = across(kv_even, 1)

    key_segs = segment_ids.reshape(2 * ranks, 1, half)
    own = segment_ids.reshape(2 * ranks, half)
    query_segs = jnp.stack(
        [
            lax.dynamic_index_in_dim(own, me, 0, keepdims=False),
            lax.dynamic_index_in_dim(own, 2 * ranks - 1 - me, 0, keepdims=False),
        ]
    )[:, :, None]
    dq, dkv_even, dkv_odd = attention(
        me.reshape(1), query_segs, key_segs, queries, grad_attn, kv_even, kv_odd, kv_here, per_kv
    )
    if special:
        input_grad, dkv_mine = paired(dq, dkv_even, dkv_odd, pieces, me, col)
    else:
        dq = dq.reshape(kv_here, 2, rows, -1).transpose(2, 0, 1, 3).reshape(rows, heads_here * HD)
        input_grad = jnp.dot(
            lax.all_gather(dq, "col", axis=1, tiled=True),
            lax.all_gather(q_weight, "row", axis=0, tiled=True),
            preferred_element_type=jnp.float32,
        ).astype(jnp.bfloat16)
        dkv_mine = chips_sum(added(dkv_even, across(dkv_odd, 1)))

    share = max(1, group // heads_here)
    if share == 1:
        parts = dkv_mine if special else [dkv_mine] + [turned(dkv_mine, k) for k in range(1, count)]
        key_grad, value_grad = by_column(col.reshape(1), parts)
        return (input_grad, key_grad, value_grad)
    whole = lax.all_gather(dkv_mine, "col")
    whole = whole.reshape(count // share, share, rows, -1).astype(jnp.float32)
    whole = whole.sum(axis=1).astype(jnp.bfloat16)
    key_grad = jnp.concatenate(list(whole[:, :, :HD]), axis=1)
    value_grad = jnp.concatenate(list(whole[:, :, HD:]), axis=1)
    return (input_grad, key_grad, value_grad)


def chips_sum(terms):
    total = terms[0].astype(jnp.float32)
    for i in range(1, terms.shape[0]):
        total += across(terms[i], 2 * i).astype(jnp.float32)
    return total.astype(jnp.bfloat16)


def paired(dq, dkv_even, dkv_odd, pieces, me, col):
    count = lax.axis_size("col")
    rows = dq.shape[2]
    core = me & 1
    side = (me >> 1) & 1

    keep_w, (send_one, send_two) = pieces[:2], pieces[2:]

    def x(block):
        return across(block, 2)

    def y(block):
        return across(block, 4)

    w_one = x(send_one)
    keep_one_y = y(keep_w[0])

    mine = lax.dynamic_index_in_dim(dq, core, 0, keepdims=False)
    theirs = across(lax.dynamic_index_in_dim(dq, 1 - core, 0, keepdims=False), 1)
    both = jnp.stack([mine, theirs], axis=1)
    keep = lax.dynamic_index_in_dim(both, side, 0, keepdims=False)
    send = lax.dynamic_index_in_dim(both, 1 - side, 0, keepdims=False)
    send, w_one, keep_one_y = tied(send, w_one, keep_one_y)
    last_one = jnp.concatenate([keep_w[1], w_one], axis=0)
    last_one_y = y(last_one)
    tokens = jnp.concatenate([keep, x(send)], axis=0)
    tokens = tokens.reshape(4 * rows, -1)
    dkv_terms = added(dkv_even, across(dkv_odd, 1))
    send_two, dkv_terms, tokens = tied(send_two, dkv_terms, tokens)
    near = [turned(tokens, 1), turned(tokens, -1)]
    w_two = x(send_two)
    dkv_x = x(dkv_terms[1::2])
    w_two_y = y(w_two)
    last_one_y, near[0], near[1] = tied(last_one_y, *near)
    cut = 2 * rows
    far = [turned(near[0][:cut], 1), turned(near[1][cut:], -1)]
    dkv_terms = added(dkv_terms[0::2], dkv_x)
    dkv_y = y(dkv_terms[1])

    pieces = [*keep_w, w_one, w_two, keep_one_y, last_one_y, w_two_y]
    sizes = [piece.shape[0] for piece in pieces]
    last = sizes[1]
    weights = [
        [(i, 0, sizes[i]) for i in (0, 1)], [(i, 0, sizes[i]) for i in (2, 3)],
        [(4, 0, sizes[4]), (5, 0, last)], [(5, last, sizes[5] - last), (6, 0, sizes[6])],
    ]
    slots = ((me >> 1) ^ ((col + jnp.arange(count)) % count)).astype(jnp.int32)
    devices = range(4)
    places = [[(k, d * rows) for d in devices] for k in range(3)]
    *most, last_weight = project(slots[2:3], slots[jnp.array([0, 1, 3])], pieces, weights, [tokens, *near], places, rows)
    *most, dkv_y = tied(*most, dkv_y)
    places = [(d // 2, d % 2 * rows) for d in devices]
    zero, one, two, three = project_rest(last_weight, far, places, rows, most)
    there = added(two, across(three, 1))
    found = across(one, 1)
    got = x(there)
    dkv_mine = added(dkv_terms[0], dkv_y)
    dkv_all = [dkv_mine] + [turned(dkv_mine, k) for k in range(1, count)]
    mine = added(zero, found)
    mine, *dkv_all = tied(mine, *dkv_all)
    return added(mine, got), dkv_all


def solution(mesh):
    placed = (
        P("row", "col"),
        P("row", None),
        P("row", None),
        P("row", "col"),
        P(),
        P("row", "col"),
    )
    return jax.shard_map(
        local,
        mesh=mesh,
        in_specs=placed,
        out_specs=(P("row", "col"), P("row", None), P("row", None)),
        check_vma=False,
    )
```
